512 devices in a mesh: cuts: 16 (over z_lo, y), space: 32 (over x, z_hi, core).
Axes of the slice: x: 4, y: 8, z: 8 (z_hi: 4, z_lo: 2; z = z_hi * 2 + z_lo), core: 2. Of those that a mesh axis runs over, the one named last changes fastest.
Arguments:
- starts: float32 [16, 3, 128, 64, 128], P('cuts', None, 'space'), may hold values from -3 to 3
Outputs:
- new_starts: float32 [16, 3, 128, 64, 128], P('cuts', None, 'space')
The draws below stay inside these ranges and needn't reach their ends.
All inputs are finite; a program needn't handle non-finite values.
Results may differ from the reference program's by a relative error of at most 0.0001.
Values sent between devices are 32-bit elements; how exact they have to be, the bound alone decides.
No kernel may reach another device: no remote copies, remote signals or barrier semaphores. Data moves between devices by JAX's collectives and lax.ppermute only.
A program may use at most 64 MiB of HBM per device.

```python
import jax
import jax.numpy as jnp
from jax import lax

NY = 64
NZ = 128
FSTEPS = 16
CSTEPS = 2
SLICES = 16
NX = 128


def steps_of(stream_key, shape, cuts, least, largest):
    loudness, own = 1.0, jax.random.fold_in(stream_key, 6)
    for axis_at, shards_of in cuts:
        draws = jnp.exp(jax.random.uniform(jax.random.fold_in(own, axis_at), (shards_of,), jnp.float32, least / len(cuts), largest / len(cuts)))
        loudness = loudness * jnp.repeat(draws, shape[axis_at] // shards_of).reshape([-1 if axis == axis_at else 1 for axis in range(len(shape))])
    return loudness


def gaussian(key, extent, scale, bound, cuts=(), kind=jnp.bfloat16):
    gain = steps_of(key, extent, cuts, -0.22, 0.18) if cuts else 1.0
    result = jax.random.normal(key, extent, jnp.float32) * scale * gain
    return jnp.minimum(jnp.maximum(result, -bound), bound).astype(kind)


def setup_inputs(seed: int = 0) -> dict:
    key_of = jax.random.split(jax.random.key(seed), 2)
    starts = gaussian(key_of[0], (SLICES, 3, NX, NY, NZ), 0.5, 3.0, ((0, 16), (2, 32)), jnp.float32)
    return {"starts": starts}


fine_rate = 0.08
fine_advect = 0.04
coarse_rate = 0.16
coarse_advect = 0.16


def advance(extended, rate, advect):
    padded = jnp.pad(extended, ((0, 0), (0, 0), (1, 1), (1, 1)))
    centre = padded[:, 1:-1, 1:-1, 1:-1]
    x_plus = padded[:, 2:, 1:-1, 1:-1]
    x_minus = padded[:, :-2, 1:-1, 1:-1]
    y_plus = padded[:, 1:-1, 2:, 1:-1]
    y_minus = padded[:, 1:-1, :-2, 1:-1]
    z_plus = padded[:, 1:-1, 1:-1, 2:]
    z_minus = padded[:, 1:-1, 1:-1, :-2]
    laplace = (x_plus + x_minus) + (y_plus + y_minus) + (z_plus + z_minus) - 6.0 * centre
    convect = centre[0:1] * (x_plus - x_minus) + centre[1:2] * (y_plus - y_minus) + centre[2:3] * (z_plus - z_minus)
    return centre + rate * laplace - advect * convect


def one_step(field, rate, advect):
    return advance(jnp.pad(field, ((0, 0), (1, 1), (0, 0), (0, 0))), rate, advect)


def fine_whole(field):
    return lax.fori_loop(0, FSTEPS, lambda index, state: one_step(state, fine_rate, fine_advect), field)


def coarse_whole(field):
    return lax.fori_loop(0, CSTEPS, lambda index, state: one_step(state, coarse_rate, coarse_advect), field)


def restrict(field):
    blocks = field.reshape(field.shape[0], field.shape[1] // 2, 2, field.shape[2] // 2, 2, field.shape[3] // 2, 2)
    return jnp.sum(blocks, axis=(2, 4, 6)) * 0.125


def prolong(field):
    return jnp.repeat(jnp.repeat(jnp.repeat(field, 2, axis=1), 2, axis=2), 2, axis=3)


def reference(starts):
    ends = lax.map(fine_whole, starts)
    old_coarse = lax.map(lambda field: coarse_whole(restrict(field)), starts)
    change = ends - lax.map(prolong, old_coarse)

    def sweep(state, previous):
        advanced = coarse_whole(state)
        corrected = prolong(advanced) + previous
        return advanced + restrict(previous), corrected

    unused, corrected = lax.scan(sweep, restrict(starts[0]), change[:-1])
    return jnp.concatenate([starts[:1], corrected], axis=0)
```

```python
import functools

import jax
import jax.numpy as jnp
from jax import lax
from jax.experimental import pallas as pl
from jax.experimental.pallas import tpu as pltpu
from jax.sharding import PartitionSpec as P

FSTEPS = 16
HALO = 4
ROUNDS = FSTEPS // HALO
NY = 64
NZ = 128
CY = NY // 4
GROUPS = 16
SLABS = 32
AXES = ("cuts", "space")
PAIRS = [[2 * k, 2 * k + 1] for k in range(SLABS // 2)]

fine_rate = 0.08
fine_advect = 0.04
coarse_rate = 0.16
coarse_advect = 0.16

VMEM = pl.BlockSpec(memory_space=pltpu.VMEM)
SMEM = pl.BlockSpec(memory_space=pltpu.SMEM)
PARAMS = pltpu.CompilerParams(vmem_limit_bytes=32 * 1024 * 1024)
f32 = jnp.float32


def one_plane(src, dst, i, o, rows, rate, advect, factor, top, bottom, left, right):
    for j in range(rows // 8):
        at = 8 + 8 * j
        mid = pl.ds(at, 8)
        v = [src[c, i, mid, :] for c in range(3)]
        av = [advect * v[c] for c in range(3)]
        xp, xm = rate - av[0], rate + av[0]
        yp, ym = rate - av[1], rate + av[1]
        zp = jnp.where(right, 0.0, rate - av[2])
        zm = jnp.where(left, 0.0, rate + av[2])
        for c in range(3):
            new = v[c] * (1.0 - 6.0 * rate)
            new += xp * src[c, i + 1, mid, :] + xm * src[c, i - 1, mid, :]
            new += yp * src[c, i, pl.ds(at + 1, 8), :] + ym * src[c, i, pl.ds(at - 1, 8), :]
            new += zp * pltpu.roll(v[c], 127, 1) + zm * pltpu.roll(v[c], 1, 1)
            dst[c, o, mid, :] = new * factor


def lanes(shape=(8, 128)):
    return lax.broadcasted_iota(jnp.int32, shape, 1)


def guards(dst, c, o, low):
    last = pltpu.roll(dst[c, o, pl.ds(CY, 8), :], 64, 1)
    first = pltpu.roll(dst[c, o, pl.ds(8, 8), :], 64, 1)
    dst[c, o, 7:8, :] = jnp.where(low, 0.0, last)[7:8, :]
    dst[c, o, CY + 8 : CY + 9, :] = jnp.where(low, first, 0.0)[0:1, :]


def coarse_step(src, dst, begin, end, limits):
    lane = lanes()
    left = (lane & 63) == 0
    right = (lane & 63) == 63
    low = lane < 64
    for i in range(begin, end):
        factor = limits(i)
        one_plane(src, dst, i, i, CY, coarse_rate, coarse_advect, factor, None, None, left, right)
        for c in range(3):
            guards(dst, c, i, low)


def fill_guards(dst, begin, end):
    low = lanes() < 64
    for i in range(begin, end):
        for c in range(3):
            guards(dst, c, i, low)


def pairs_to_one(scale):
    rows = lax.broadcasted_iota(jnp.int32, (256, 128), 0)
    columns = lax.broadcasted_iota(jnp.int32, (256, 128), 1)
    return jnp.where((rows >> 1) == columns, f32(scale), f32(0.0))


def one_to_pairs():
    rows = lax.broadcasted_iota(jnp.int32, (128, 256), 0)
    columns = lax.broadcasted_iota(jnp.int32, (128, 256), 1)
    return jnp.where(rows == (columns >> 1), f32(1.0), f32(0.0))


def dot(a, b):
    return jnp.dot(a, b, precision=lax.Precision.HIGHEST, preferred_element_type=f32)


def restricted(planes):
    def rows(c, p):
        total = (planes(c, 2 * p, 0) + planes(c, 2 * p, 1)) + (planes(c, 2 * p + 1, 0) + planes(c, 2 * p + 1, 1))
        return jnp.concatenate([total[:CY], total[CY:]], axis=1)

    return rows


def fine_kernel(last, flags, left_ref, mid_ref, right_ref, *rest):
    if last:
        oc_ref, out_ref, q_ref, a, b, sums = rest
    else:
        out_ref, a, b = rest
    lane = lanes()
    left = lane == 0
    right = lane == 127
    zero = jnp.zeros((8, 128), f32)
    for c in range(3):

        def clear(i, carry):
            for buffer in (a, b):
                buffer[c, i, 0:8, :] = zero
                buffer[c, i, NY + 8 : NY + 16, :] = zero
            return carry

        lax.fori_loop(0, 3 * HALO, clear, 0)
        for at, ref in ((0, left_ref), (HALO, mid_ref), (2 * HALO, right_ref)):
            for i in range(HALO):
                a[c, at + i, 8 : NY + 8, :] = ref[c, i]
    has_left = flags[0].astype(f32)
    has_right = flags[1].astype(f32)
    src, dst = a, b
    for step in range(1, HALO + 1):

        def plane(i, carry):
            factor = jnp.where(i < HALO, has_left, jnp.where(i >= 2 * HALO, has_right, 1.0))
            one_plane(src, dst, i, i, NY, fine_rate, fine_advect, factor, None, None, left, right)
            return carry

        lax.fori_loop(step, 3 * HALO - step, plane, 0)
        src, dst = dst, src
    for c in range(3):
        for i in range(HALO):
            out_ref[c, i] = src[c, HALO + i, 8 : NY + 8, :]
    if last:
        rows = restricted(lambda c, p, start: src[c, HALO + p, pl.ds(8 + start, 32, stride=2), :])
        for c in range(3):
            for p in range(2):
                sums[pl.ds((c * 2 + p) * CY, CY), :] = rows(c, p)
        ended = dot(sums[...], pairs_to_one(0.125))
        keep = jnp.where(flags[2] == 0, 0.0, 1.0)
        for c in range(3):
            for p in range(2):
                at = (c * 2 + p) * CY
                q_ref[c, p] = ended[at : at + CY] - keep * oc_ref[c, p]


def fine_round(flags, left, mid, right, oc=None):
    last = oc is not None
    shape = jax.ShapeDtypeStruct(mid.shape, f32)
    buffer = pltpu.VMEM((3, 3 * HALO, NY + 16, NZ), f32)
    coarse = jax.ShapeDtypeStruct((3, 2, CY, NZ), f32)
    return pl.pallas_call(
        functools.partial(fine_kernel, last),
        out_shape=(shape, coarse) if last else shape,
        in_specs=[SMEM] + [VMEM] * (4 if last else 3),
        out_specs=(VMEM, VMEM) if last else VMEM,
        scratch_shapes=[buffer, buffer] + ([pltpu.VMEM((6 * CY, 256), f32)] if last else []),
        compiler_params=PARAMS,
        cost_estimate=pl.CostEstimate(flops=40_000_000, bytes_accessed=2_000_000, transcendentals=0),
        name="fine_last" if last else "fine_steps",
    )(flags, left, mid, right, *([oc] if last else []))


def first_coarse_kernel(flags, left_ref, mid_ref, right_ref, out_ref, a, b, sums):
    for c in range(3):
        for part, ref in enumerate((left_ref, mid_ref, right_ref)):
            rows = restricted(lambda c, p, start: ref[c, p, pl.ds(start, 32, stride=2), :])
            for p in range(2):
                sums[pl.ds((c * 6 + part * 2 + p) * CY, CY), :] = rows(c, p)
    averaged = dot(sums[...], pairs_to_one(0.125))
    for c in range(3):
        for i in range(6):
            at = (c * 6 + i) * CY
            a[c, i, 8 : CY + 8, :] = averaged[at : at + CY]
    fill_guards(a, 0, 6)
    has_left = flags[0].astype(f32)
    has_right = flags[1].astype(f32)
    limits = lambda i: has_left if i < 2 else has_right if i >= 4 else f32(1.0)
    coarse_step(a, b, 1, 5, limits)
    coarse_step(b, a, 2, 4, limits)
    for c in range(3):
        for i in range(2):
            out_ref[c, i] = a[c, 2 + i, 8 : CY + 8, :]


def first_coarse(flags, left, mid, right):
    buffer = pltpu.VMEM((3, 6, CY + 16, NZ), f32)
    return pl.pallas_call(
        first_coarse_kernel,
        out_shape=jax.ShapeDtypeStruct((3, 2, CY, NZ), f32),
        in_specs=[SMEM, VMEM, VMEM, VMEM],
        out_specs=VMEM,
        scratch_shapes=[buffer, buffer, pltpu.VMEM((18 * CY, 256), f32)],
        compiler_params=PARAMS,
        cost_estimate=pl.CostEstimate(flops=4_000_000, bytes_accessed=1_300_000, transcendentals=0),
        name="first_coarse",
    )(flags, left, mid, right)


def change_kernel(ends_ref, oc_ref, out_ref):
    expand = one_to_pairs()
    for c in range(3):
        for p in range(2):
            wide = dot(oc_ref[c, p], expand)
            tall = jnp.concatenate([wide[:, :NZ], wide[:, NZ:]], axis=0)
            for i in (2 * p, 2 * p + 1):
                for start in (0, 1):
                    at = pl.ds(start, 32, stride=2)
                    out_ref[c, i, at, :] = ends_ref[c, i, at, :] - tall


def fine_change(ends, oc):
    return pl.pallas_call(
        change_kernel,
        out_shape=jax.ShapeDtypeStruct(ends.shape, f32),
        in_specs=[VMEM, VMEM],
        out_specs=VMEM,
        compiler_params=PARAMS,
        cost_estimate=pl.CostEstimate(flops=1_000_000, bytes_accessed=900_000, transcendentals=0),
        name="fine_change",
    )(ends, oc)


def sweep_kernel(turn, flags, got_ref, before_ref, d_left, d_mid, d_right, d_own, even_ref, odd_ref, s_ref, even_out, odd_out, a, b):
    for c in range(3):
        for core in range(2):
            for i in range(4):
                a[c, 8 * core + i, 8 : CY + 8, :] = got_ref[core, c, i]
            for i in range(2):
                a[c, 4 + 2 * core + i, 8 : CY + 8, :] = before_ref[core, c, i]
    fill_guards(a, 0, 12)
    has_left = flags[3].astype(f32)
    has_right = flags[4].astype(f32)
    core = flags[5]
    mine = flags[2] == 2 * turn
    limits = lambda i: has_left if i < 4 else has_right if i >= 8 else f32(1.0)
    coarse_step(a, b, 1, 11, limits)
    coarse_step(b, a, 2, 10, limits)
    for c in range(3):
        for i in range(2):
            first = jnp.where(core == 0, a[c, 4 + i, 8 : CY + 8, :], a[c, 6 + i, 8 : CY + 8, :])
            even_out[c, i] = jnp.where(mine, first, even_ref[c, i])
        for i, part in enumerate([d_left.at[c, 0], d_left.at[c, 1]] + [d_mid.at[c, k] for k in range(4)] + [d_right.at[c, 0], d_right.at[c, 1]]):
            a[c, 2 + i, 8 : CY + 8, :] += part[...]
    fill_guards(a, 2, 10)
    coarse_step(a, b, 3, 9, limits)
    coarse_step(b, a, 4, 8, limits)
    for c in range(3):
        for i in range(4):
            s_ref[c, i] = a[c, 4 + i, 8 : CY + 8, :] + d_own[c, i]
        for i in range(2):
            second = jnp.where(core == 0, a[c, 4 + i, 8 : CY + 8, :], a[c, 6 + i, 8 : CY + 8, :])
            odd_out[c, i] = jnp.where(mine, second, odd_ref[c, i])


def sweep(turn, flags, *arrays):
    buffer = pltpu.VMEM((3, 12, CY + 16, NZ), f32)
    two = jax.ShapeDtypeStruct((3, 2, CY, NZ), f32)
    four = jax.ShapeDtypeStruct((3, 4, CY, NZ), f32)
    return pl.pallas_call(
        functools.partial(sweep_kernel, turn),
        out_shape=(four, two, two),
        in_specs=[SMEM] + [VMEM] * len(arrays),
        out_specs=(VMEM,) * 3,
        scratch_shapes=[buffer, buffer],
        compiler_params=PARAMS,
        cost_estimate=pl.CostEstimate(flops=4_000_000, bytes_accessed=900_000, transcendentals=0),
        name="sweep",
    )(flags, *arrays)


def final_kernel(flags, start_ref, previous_ref, even_ref, odd_ref, out_ref):
    group = flags[2]

    @pl.when(group == 0)
    def _():
        out_ref[...] = start_ref[...]

    @pl.when(group != 0)
    def _():
        expand = one_to_pairs()
        odd = (group & 1) == 1
        for c in range(3):
            for p in range(2):
                wide = dot(jnp.where(odd, odd_ref[c, p], even_ref[c, p]), expand)
                tall = jnp.concatenate([wide[:, :NZ], wide[:, NZ:]], axis=0)
                for i in (2 * p, 2 * p + 1):
                    for start in (0, 1):
                        at = pl.ds(start, 32, stride=2)
                        out_ref[c, i, at, :] = previous_ref[c, i, at, :] + tall


def final(flags, start, previous, even, odd):
    return pl.pallas_call(
        final_kernel,
        out_shape=jax.ShapeDtypeStruct(start.shape, f32),
        in_specs=[SMEM] + [VMEM] * 4,
        out_specs=VMEM,
        compiler_params=PARAMS,
        cost_estimate=pl.CostEstimate(flops=1_000_000, bytes_accessed=1_300_000, transcendentals=0),
        name="final",
    )(flags, start, previous, even, odd)


def handed_on(value, groups, by, place):
    table = []
    for c in groups:
        if not 0 <= c + by < GROUPS:
            continue
        for s in range(SLABS):
            if 0 <= place(s) < SLABS:
                table.append((c * SLABS + s, (c + by) * SLABS + place(s)))
    return lax.ppermute(value, AXES, table)


def both_cores(value):
    return lax.all_gather(value, "space", axis=0, tiled=False, axis_index_groups=PAIRS)


def shards(starts):
    initial = starts[0]
    group = lax.axis_index("cuts")
    slab = lax.axis_index("space")
    flags = jnp.stack(
        [slab > 0, slab < SLABS - 1, group, slab > 1, slab < SLABS - 2, slab & 1, group, group]
    ).astype(jnp.int32)
    up = [(s, s + 1) for s in range(SLABS - 1)]
    down = [(s + 1, s) for s in range(SLABS - 1)]
    field = initial
    for turn in range(ROUNDS):
        left = lax.ppermute(field, "space", up)
        right = lax.ppermute(field, "space", down)
        if turn == 0:
            oc = first_coarse(flags, left, field, right)
        if turn < ROUNDS - 1:
            field = fine_round(flags, left, field, right)
        else:
            ends, mine = fine_round(flags, left, field, right, oc)
    pair = both_cores(mine)
    whole = jnp.concatenate([pair[0], pair[1]], axis=1)
    odd_groups = range(1, GROUPS, 2)
    even_groups = range(0, GROUPS, 2)
    core = slab & 1
    state, even, odd = whole, oc, oc
    for turn in range(1, GROUPS // 2):
        outer = handed_on(state, [2 * turn - 2], 2, lambda s: s + 2 if s % 2 == 0 else s - 2)
        half = jnp.where(core == 0, state[:, :2], state[:, 2:])
        inner = handed_on(half, [2 * turn - 2], 2, lambda s: s)
        if turn == 1:
            d_left = handed_on(whole[:, 2:], odd_groups, 1, lambda s: s + 2)
            d_right = handed_on(whole[:, :2], odd_groups, 1, lambda s: s - 2)
            d_mid = handed_on(whole, odd_groups, 1, lambda s: s)
        both = both_cores(jnp.concatenate([outer, inner], axis=1))
        state, even, odd = sweep(turn, flags, both[:, :, :4], both[:, :, 4:], d_left, d_mid, d_right, whole, even, odd)
        if turn == 1:
            change = fine_change(ends, oc)
            change, state = lax.optimization_barrier((change, state))
            previous = handed_on(change, range(GROUPS), 1, lambda s: s)
    filled = handed_on(odd, even_groups, 1, lambda s: s)
    return final(flags, initial, previous, even, filled)[None]


def solution(mesh):
    placed = P("cuts", None, "space", None, None)
    return jax.shard_map(shards, mesh=mesh, in_specs=(placed,), out_specs=placed, check_vma=False)
```

```python
import functools

import jax
import jax.numpy as jnp
from jax import lax
from jax.experimental import pallas as pl
from jax.experimental.pallas import tpu as pltpu
from jax.sharding import PartitionSpec as P

FSTEPS = 16
HALO = 4
ROUNDS = FSTEPS // HALO
NY = 64
NZ = 128
CY = NY // 4
GROUPS = 16
SLABS = 32
AXES = ("cuts", "space")
PAIRS = [[2 * k, 2 * k + 1] for k in range(SLABS // 2)]

fine_rate = 0.08
fine_advect = 0.04
coarse_rate = 0.16
coarse_advect = 0.16

VMEM = pl.BlockSpec(memory_space=pltpu.VMEM)
PARAMS = pltpu.CompilerParams(vmem_limit_bytes=32 * 1024 * 1024)
f32 = jnp.float32


def position():
    return lax.axis_index("cuts"), lax.axis_index("space")


def one_plane(src, dst, i, rows, rate, advect, factor, left, right):
    edge = []
    for j in range(rows // 8):
        at = 8 + 8 * j
        mid = pl.ds(at, 8)
        v = [src[c, i, mid, :] for c in range(3)]
        av = [advect * v[c] for c in range(3)]
        xp, xm = rate - av[0], rate + av[0]
        yp, ym = rate - av[1], rate + av[1]
        zp = jnp.where(right, 0.0, rate - av[2])
        zm = jnp.where(left, 0.0, rate + av[2])
        row = []
        for c in range(3):
            new = v[c] * (1.0 - 6.0 * rate)
            new += xp * src[c, i + 1, mid, :] + xm * src[c, i - 1, mid, :]
            new += yp * src[c, i, pl.ds(at + 1, 8), :] + ym * src[c, i, pl.ds(at - 1, 8), :]
            new += zp * pltpu.roll(v[c], 127, 1) + zm * pltpu.roll(v[c], 1, 1)
            if factor is not None:
                new = new * factor
            dst[c, i, mid, :] = new
            row.append(new)
        edge.append(row)
    return edge[0], edge[-1]


def lanes(shape=(8, 128)):
    return lax.broadcasted_iota(jnp.int32, shape, 1)


def guards(dst, c, i, first, last, low):
    dst[c, i, 7:8, :] = jnp.where(low, 0.0, pltpu.roll(last, 64, 1))[7:8, :]
    dst[c, i, CY + 8 : CY + 9, :] = jnp.where(low, pltpu.roll(first, 64, 1), 0.0)[0:1, :]


def put_coarse(dst, c, i, plane, low):
    dst[c, i, 8 : CY + 8, :] = plane
    guards(dst, c, i, plane[:8], plane[8:], low)


def coarse_step(src, dst, begin, end, limits, guarded=True):
    lane = lanes()
    left = (lane & 63) == 0
    right = (lane & 63) == 63
    low = lane < 64
    for i in range(begin, end):
        first, last = one_plane(src, dst, i, CY, coarse_rate, coarse_advect, limits(i), left, right)
        if guarded:
            for c in range(3):
                guards(dst, c, i, first[c], last[c], low)


def pairs_to_one(scale):
    rows = lax.broadcasted_iota(jnp.int32, (256, 128), 0)
    columns = lax.broadcasted_iota(jnp.int32, (256, 128), 1)
    return jnp.where((rows >> 1) == columns, f32(scale), f32(0.0))


def one_to_pairs():
    rows = lax.broadcasted_iota(jnp.int32, (128, 256), 0)
    columns = lax.broadcasted_iota(jnp.int32, (128, 256), 1)
    return jnp.where(rows == (columns >> 1), f32(1.0), f32(0.0))


def dot(a, b):
    return jnp.dot(a, b, precision=lax.Precision.HIGHEST, preferred_element_type=f32)


def restricted(planes):
    def rows(c, p):
        total = (planes(c, 2 * p, 0) + planes(c, 2 * p, 1)) + (planes(c, 2 * p + 1, 0) + planes(c, 2 * p + 1, 1))
        return jnp.concatenate([total[:CY], total[CY:]], axis=1)

    return rows


def fine_kernel(last, left_ref, mid_ref, right_ref, *rest):
    if last:
        oc_ref, out_ref, q_ref, a, b, sums = rest
    else:
        out_ref, a, b = rest
    group, slab = position()
    lane = lanes()
    left = lane == 0
    right = lane == 127
    zero = jnp.zeros((8, 128), f32)
    for c in range(3):
        for i in range(3 * HALO):
            for buffer in (a, b):
                buffer[c, i, 0:8, :] = zero
                buffer[c, i, NY + 8 : NY + 16, :] = zero
        for at, ref in ((0, left_ref), (HALO, mid_ref), (2 * HALO, right_ref)):
            for i in range(HALO):
                a[c, at + i, 8 : NY + 8, :] = ref[c, i]
    has_left = jnp.where(slab > 0, f32(1.0), f32(0.0))
    has_right = jnp.where(slab < SLABS - 1, f32(1.0), f32(0.0))
    src, dst = a, b
    for step in range(1, HALO + 1):
        for i in range(step, 3 * HALO - step):
            factor = has_left if i < HALO else has_right if i >= 2 * HALO else None
            one_plane(src, dst, i, NY, fine_rate, fine_advect, factor, left, right)
        src, dst = dst, src
    for c in range(3):
        for i in range(HALO):
            out_ref[c, i] = src[c, HALO + i, 8 : NY + 8, :]
    if last:
        rows = restricted(lambda c, p, start: src[c, HALO + p, pl.ds(8 + start, 32, stride=2), :])
        for c in range(3):
            for p in range(2):
                sums[pl.ds((c * 2 + p) * CY, CY), :] = rows(c, p)
        ended = dot(sums[...], pairs_to_one(0.125))
        keep = jnp.where(group == 0, f32(0.0), f32(1.0))
        for c in range(3):
            for p in range(2):
                at = (c * 2 + p) * CY
                q_ref[c, p] = ended[at : at + CY] - keep * oc_ref[c, p]


def fine_round(left, mid, right, oc=None):
    last = oc is not None
    shape = jax.ShapeDtypeStruct(mid.shape, f32)
    buffer = pltpu.VMEM((3, 3 * HALO, NY + 16, NZ), f32)
    coarse = jax.ShapeDtypeStruct((3, 2, CY, NZ), f32)
    return pl.pallas_call(
        functools.partial(fine_kernel, last),
        out_shape=(shape, coarse) if last else shape,
        in_specs=[VMEM] * (4 if last else 3),
        out_specs=(VMEM, VMEM) if last else VMEM,
        scratch_shapes=[buffer, buffer] + ([pltpu.VMEM((6 * CY, 256), f32)] if last else []),
        compiler_params=PARAMS,
        cost_estimate=pl.CostEstimate(flops=40_000_000, bytes_accessed=2_000_000, transcendentals=0),
        name="fine_last" if last else "fine_steps",
    )(left, mid, right, *([oc] if last else []))


def first_coarse_kernel(left_ref, mid_ref, right_ref, out_ref, a, b, sums):
    group, slab = position()
    for c in range(3):
        for part, ref in enumerate((left_ref, mid_ref, right_ref)):
            rows = restricted(lambda c, p, start: ref[c, p, pl.ds(start, 32, stride=2), :])
            for p in range(2):
                sums[pl.ds((c * 6 + part * 2 + p) * CY, CY), :] = rows(c, p)
    averaged = dot(sums[...], pairs_to_one(0.125))
    low = lanes() < 64
    for c in range(3):
        for i in range(6):
            at = (c * 6 + i) * CY
            put_coarse(a, c, i, averaged[at : at + CY], low)
    has_left = jnp.where(slab > 0, f32(1.0), f32(0.0))
    has_right = jnp.where(slab < SLABS - 1, f32(1.0), f32(0.0))
    limits = lambda i: has_left if i < 2 else has_right if i >= 4 else None
    coarse_step(a, b, 1, 5, limits)
    coarse_step(b, a, 2, 4, limits, False)
    for c in range(3):
        for i in range(2):
            out_ref[c, i] = a[c, 2 + i, 8 : CY + 8, :]


def first_coarse(left, mid, right):
    buffer = pltpu.VMEM((3, 6, CY + 16, NZ), f32)
    return pl.pallas_call(
        first_coarse_kernel,
        out_shape=jax.ShapeDtypeStruct((3, 2, CY, NZ), f32),
        in_specs=[VMEM, VMEM, VMEM],
        out_specs=VMEM,
        scratch_shapes=[buffer, buffer, pltpu.VMEM((18 * CY, 256), f32)],
        compiler_params=PARAMS,
        cost_estimate=pl.CostEstimate(flops=4_000_000, bytes_accessed=1_300_000, transcendentals=0),
        name="first_coarse",
    )(left, mid, right)


def change_kernel(ends_ref, oc_ref, out_ref):
    expand = one_to_pairs()
    for c in range(3):
        for p in range(2):
            wide = dot(oc_ref[c, p], expand)
            tall = jnp.concatenate([wide[:, :NZ], wide[:, NZ:]], axis=0)
            for i in (2 * p, 2 * p + 1):
                for start in (0, 1):
                    at = pl.ds(start, 32, stride=2)
                    out_ref[c, i, at, :] = ends_ref[c, i, at, :] - tall


def fine_change(ends, oc):
    return pl.pallas_call(
        change_kernel,
        out_shape=jax.ShapeDtypeStruct(ends.shape, f32),
        in_specs=[VMEM, VMEM],
        out_specs=VMEM,
        compiler_params=PARAMS,
        cost_estimate=pl.CostEstimate(flops=1_000_000, bytes_accessed=900_000, transcendentals=0),
        name="fine_change",
    )(ends, oc)


def halves(count):
    outer = count - 2
    first = min(outer, 4)
    for i in range(first):
        yield 0, i, outer - first + i
        yield 1, i, outer + 4 + i
    for i in range(outer - first):
        yield 0, first + i, i
        yield 1, first + i, outer + 4 + first + i
    for i in range(2):
        yield 0, outer + i, outer + i
        yield 1, outer + i, outer + 2 + i


def sweep_kernel(target, depth, *refs):
    got_ref, before_ref, own_ref, *kept = refs[: 3 + depth]
    state_ref, *results = refs[3 + depth : 4 + 2 * depth]
    a, b = refs[4 + 2 * depth :]
    group, slab = position()
    core = slab & 1
    mine = group == target
    low = lanes() < 64
    reach = 2 * depth
    width = 2 * reach + 4
    for core_at, at, place in halves(reach + 2):
        for c in range(3):
            put_coarse(a, c, place, got_ref[core_at, c, at], low)
    chip = slab >> 1
    inside = {}
    for k in range(-reach, reach + 4):
        block = k // 4
        if block not in inside:
            there = chip + block
            inside[block] = None if block == 0 else jnp.where((there >= 0) & (there < SLABS // 2), f32(1.0), f32(0.0))
    limits = lambda i: inside[(i - reach) // 4]
    at_before = 0
    for turn in range(depth):
        edge = 2 * turn
        final_turn = turn == depth - 1
        coarse_step(a, b, edge + 1, width - edge - 1, limits)
        coarse_step(b, a, edge + 2, width - edge - 2, limits, False)
        for c in range(3):
            for i in range(2):
                value = jnp.where(core == 0, a[c, reach + i, 8 : CY + 8, :], a[c, reach + 2 + i, 8 : CY + 8, :])
                results[turn][c, i] = jnp.where(mine, value, kept[turn][c, i])
        if final_turn:
            for c in range(3):
                for i in range(4):
                    state_ref[c, i] = a[c, reach + i, 8 : CY + 8, :] + own_ref[c, i]
        else:
            count = reach - edge
            for core_at, at, place in halves(count):
                for c in range(3):
                    i = place + edge + 2
                    put_coarse(a, c, i, a[c, i, 8 : CY + 8, :] + before_ref[core_at, c, at_before + at], low)
            at_before += count


def sweep(target, depth, got, before, own, kept):
    buffer = pltpu.VMEM((3, 4 * depth + 4, CY + 16, NZ), f32)
    two = jax.ShapeDtypeStruct((3, 2, CY, NZ), f32)
    four = jax.ShapeDtypeStruct((3, 4, CY, NZ), f32)
    return pl.pallas_call(
        functools.partial(sweep_kernel, target, depth),
        out_shape=(four,) + (two,) * depth,
        in_specs=[VMEM] * (3 + depth),
        out_specs=(VMEM,) * (1 + depth),
        scratch_shapes=[buffer, buffer],
        compiler_params=PARAMS,
        cost_estimate=pl.CostEstimate(flops=4_000_000, bytes_accessed=900_000, transcendentals=0),
        name="sweep_%d" % depth,
    )(got, before, own, *kept)


def final_kernel(start_ref, previous_ref, own_ref, a_ref, b_ref, c_ref, out_ref):
    group, slab = position()

    @pl.when(group == 0)
    def _():
        out_ref[...] = start_ref[...]

    @pl.when(group != 0)
    def _():
        expand = one_to_pairs()
        chain = (group & 3) == 2
        for c in range(3):
            for p in range(2):
                others = a_ref[c, p] + b_ref[c, p] + c_ref[c, p]
                wide = dot(jnp.where(chain, own_ref[c, p], others), expand)
                tall = jnp.concatenate([wide[:, :NZ], wide[:, NZ:]], axis=0)
                for i in (2 * p, 2 * p + 1):
                    for start in (0, 1):
                        at = pl.ds(start, 32, stride=2)
                        out_ref[c, i, at, :] = previous_ref[c, i, at, :] + tall


def final(*arrays):
    return pl.pallas_call(
        final_kernel,
        out_shape=jax.ShapeDtypeStruct(arrays[0].shape, f32),
        in_specs=[VMEM] * len(arrays),
        out_specs=VMEM,
        compiler_params=PARAMS,
        cost_estimate=pl.CostEstimate(flops=1_000_000, bytes_accessed=1_300_000, transcendentals=0),
        name="final",
    )(*arrays)


def handed_on(value, groups, by, place):
    table = []
    for c in groups:
        for s in range(SLABS):
            if 0 <= place(s) < SLABS and 0 <= c + by < GROUPS:
                table.append((c * SLABS + s, (c + by) * SLABS + place(s)))
    return lax.ppermute(value, AXES, table)


def outward(chips):
    return lambda s: s + 2 * chips if s % 2 == 0 else s - 2 * chips


def here(s):
    return s


def both_cores(value):
    return lax.all_gather(value, "space", axis=0, tiled=False, axis_index_groups=PAIRS)


def joined(*parts):
    return jnp.concatenate(parts, axis=1)


def after(value, *others):
    return lax.optimization_barrier((value, *others))[0]


def shards(starts):
    initial = starts[0]
    slab = lax.axis_index("space")
    core = slab & 1
    up = [(s, s + 1) for s in range(SLABS - 1)]
    down = [(s + 1, s) for s in range(SLABS - 1)]
    field = initial
    for turn in range(ROUNDS):
        left = lax.ppermute(field, "space", up)
        right = lax.ppermute(field, "space", down)
        if turn == 0:
            oc = first_coarse(left, field, right)
        if turn < ROUNDS - 1:
            field = fine_round(left, field, right)
        else:
            ends, mine = fine_round(left, field, right, oc)
    pair = both_cores(mine)
    whole = joined(pair[0], pair[1])

    def near(value):
        return jnp.where(core == 0, value[:, 2:4], value[:, 0:2])

    s1 = handed_on(whole, [0], 2, outward(1))
    s0 = handed_on(mine, [0], 2, here)
    d1 = handed_on(near(whole), [1], 1, outward(1))
    d0 = handed_on(mine, [1], 1, here)
    sources = [c for c in range(3, GROUPS - 2) if c % 4 != 2]
    l1 = handed_on(whole, sources, 0, outward(1))
    l2 = handed_on(near(whole), sources[::3], 0, outward(2))
    y3 = handed_on(joined(l1, l2, mine), sources[::3], 3, here)
    y2 = handed_on(joined(l1, mine), sources[1::3], 2, here)
    y1 = handed_on(joined(near(l1), mine), sources[2::3], 1, here)
    before = both_cores(joined(y3, y2, y1))
    change = after(fine_change(ends, oc), before)
    previous = handed_on(change, range(GROUPS), 1, here)
    s1 = after(s1, before)
    both = both_cores(joined(s1, s0, d1, d0))
    state, own, plus = sweep(2, 2, both[:, :, :6], both[:, :, 6:], whole, (oc, oc))
    minus2 = minus1 = oc
    for target in (6, 10, 14):
        half = jnp.where(core == 0, state[:, :2], state[:, 2:])
        s2 = handed_on(state, [target - 4], 4, outward(2))
        s1 = handed_on(state, [target - 4], 4, outward(1))
        s0 = handed_on(half, [target - 4], 4, here)
        both = both_cores(joined(s1, s2, s0))
        state, minus2, minus1, own, plus = sweep(target, 4, both, before, whole, (minus2, minus1, own, plus))
    plus = handed_on(plus, [0, 2, 6, 10, 14], 1, here)
    minus1 = handed_on(minus1, [6, 10, 14], -1, here)
    minus2 = handed_on(minus2, [6, 10, 14], -2, here)
    return final(initial, previous, own, plus, minus1, minus2)[None]


def solution(mesh):
    placed = P("cuts", None, "space", None, None)
    return jax.shard_map(shards, mesh=mesh, in_specs=(placed,), out_specs=placed, check_vma=False)
```

```python
import functools

import jax
import jax.numpy as jnp
from jax import lax
from jax.experimental import pallas as pl
from jax.experimental.pallas import tpu as pltpu
from jax.sharding import PartitionSpec as P

FSTEPS = 16
HALO = 4
ROUNDS = FSTEPS // HALO
NY = 64
NZ = 128
CY = NY // 4
GROUPS = 16
SLABS = 32
AXES = ("cuts", "space")
PAIRS = [[2 * k, 2 * k + 1] for k in range(SLABS // 2)]

fine_rate = 0.08
fine_advect = 0.04
coarse_rate = 0.16
coarse_advect = 0.16

VMEM = pl.BlockSpec(memory_space=pltpu.VMEM)
PARAMS = pltpu.CompilerParams(vmem_limit_bytes=32 * 1024 * 1024)
f32 = jnp.float32


def position():
    return lax.axis_index("cuts"), lax.axis_index("space")


def one_plane(src, dst, i, rows, rate, advect, factor, left, right):
    edge = []
    for j in range(rows // 8):
        at = 8 + 8 * j
        mid = pl.ds(at, 8)
        v = [src[c, i, mid, :] for c in range(3)]
        av = [advect * v[c] for c in range(3)]
        xp, xm = rate - av[0], rate + av[0]
        yp, ym = rate - av[1], rate + av[1]
        zp = jnp.where(right, 0.0, rate - av[2])
        zm = jnp.where(left, 0.0, rate + av[2])
        row = []
        for c in range(3):
            new = v[c] * (1.0 - 6.0 * rate)
            new += xp * src[c, i + 1, mid, :] + xm * src[c, i - 1, mid, :]
            new += yp * src[c, i, pl.ds(at + 1, 8), :] + ym * src[c, i, pl.ds(at - 1, 8), :]
            new += zp * pltpu.roll(v[c], 127, 1) + zm * pltpu.roll(v[c], 1, 1)
            if factor is not None:
                new = new * factor
            dst[c, i, mid, :] = new
            row.append(new)
        edge.append(row)
    return edge[0], edge[-1]


def lanes(shape=(8, 128)):
    return lax.broadcasted_iota(jnp.int32, shape, 1)


def coarse_plane(at, put, i, factor):
    lane = lanes()
    row = lax.broadcasted_iota(jnp.int32, (8, 128), 0)
    z_first, z_last = (lane & 63) == 0, (lane & 63) == 63
    y_first, y_last = (row == 0) & (lane < 64), (row == 7) & (lane >= 64)
    row_first, row_last = row == 0, row == 7
    v = [[at(c, i, j) for j in range(2)] for c in range(3)]
    for j in range(2):
        av = [coarse_advect * v[c][j] for c in range(3)]
        xp, xm = coarse_rate - av[0], coarse_rate + av[0]
        yp, ym = coarse_rate - av[1], coarse_rate + av[1]
        if j == 0:
            ym = jnp.where(y_first, 0.0, ym)
        else:
            yp = jnp.where(y_last, 0.0, yp)
        zp = jnp.where(z_last, 0.0, coarse_rate - av[2])
        zm = jnp.where(z_first, 0.0, coarse_rate + av[2])
        for c in range(3):
            here_, other = v[c][j], v[c][1 - j]
            swapped = pltpu.roll(other, 64, 1)
            below = jnp.where(row_last, swapped if j == 0 else other, here_)
            above = jnp.where(row_first, other if j == 0 else swapped, here_)
            new = here_ * (1.0 - 6.0 * coarse_rate)
            new += xp * at(c, i + 1, j) + xm * at(c, i - 1, j)
            new += yp * pltpu.roll(above, 7, 0) + ym * pltpu.roll(below, 1, 0)
            new += zp * pltpu.roll(here_, 127, 1) + zm * pltpu.roll(here_, 1, 1)
            if factor is not None:
                new = new * factor
            put(c, i, j, new)


def reads(ref):
    return lambda c, i, j: ref[c, i, 8 * j : 8 * j + 8, :]


def writes(ref):
    def put(c, i, j, value):
        ref[c, i, 8 * j : 8 * j + 8, :] = value

    return put


def coarse_step(at, put, begin, end, limits):
    for i in range(begin, end):
        coarse_plane(at, put, i, limits(i))


def pairs_to_one(scale):
    rows = lax.broadcasted_iota(jnp.int32, (256, 128), 0)
    columns = lax.broadcasted_iota(jnp.int32, (256, 128), 1)
    return jnp.where((rows >> 1) == columns, f32(scale), f32(0.0))


def one_to_pairs():
    rows = lax.broadcasted_iota(jnp.int32, (128, 256), 0)
    columns = lax.broadcasted_iota(jnp.int32, (128, 256), 1)
    return jnp.where(rows == (columns >> 1), f32(1.0), f32(0.0))


def dot(a, b):
    return jnp.dot(a, b, precision=lax.Precision.HIGHEST, preferred_element_type=f32)


def restricted(planes):
    def rows(c, p):
        total = (planes(c, 2 * p, 0) + planes(c, 2 * p, 1)) + (planes(c, 2 * p + 1, 0) + planes(c, 2 * p + 1, 1))
        return jnp.concatenate([total[:CY], total[CY:]], axis=1)

    return rows


def fine_kernel(last, left_ref, mid_ref, right_ref, *rest):
    if last:
        oc_ref, out_ref, q_ref, a, b, sums = rest
    else:
        out_ref, a, b = rest
    group, slab = position()
    lane = lanes()
    left = lane == 0
    right = lane == 127
    zero = jnp.zeros((8, 128), f32)
    for c in range(3):
        for i in range(3 * HALO):
            for buffer in (a, b):
                buffer[c, i, 0:8, :] = zero
                buffer[c, i, NY + 8 : NY + 16, :] = zero
        for at, ref in ((0, left_ref), (HALO, mid_ref), (2 * HALO, right_ref)):
            for i in range(HALO):
                a[c, at + i, 8 : NY + 8, :] = ref[c, i]
    has_left = jnp.where(slab > 0, f32(1.0), f32(0.0))
    has_right = jnp.where(slab < SLABS - 1, f32(1.0), f32(0.0))
    src, dst = a, b
    for step in range(1, HALO + 1):
        for i in range(step, 3 * HALO - step):
            factor = has_left if i < HALO else has_right if i >= 2 * HALO else None
            one_plane(src, dst, i, NY, fine_rate, fine_advect, factor, left, right)
        src, dst = dst, src
    for c in range(3):
        for i in range(HALO):
            out_ref[c, i] = src[c, HALO + i, 8 : NY + 8, :]
    if last:
        rows = restricted(lambda c, p, start: src[c, HALO + p, pl.ds(8 + start, 32, stride=2), :])
        for c in range(3):
            for p in range(2):
                sums[pl.ds((c * 2 + p) * CY, CY), :] = rows(c, p)
        ended = dot(sums[...], pairs_to_one(0.125))
        keep = jnp.where(group == 0, f32(0.0), f32(1.0))
        for c in range(3):
            for p in range(2):
                at = (c * 2 + p) * CY
                q_ref[c, p] = ended[at : at + CY] - keep * oc_ref[c, p]


def fine_round(left, mid, right, oc=None):
    last = oc is not None
    shape = jax.ShapeDtypeStruct(mid.shape, f32)
    buffer = pltpu.VMEM((3, 3 * HALO, NY + 16, NZ), f32)
    coarse = jax.ShapeDtypeStruct((3, 2, CY, NZ), f32)
    return pl.pallas_call(
        functools.partial(fine_kernel, last),
        out_shape=(shape, coarse) if last else shape,
        in_specs=[VMEM] * (4 if last else 3),
        out_specs=(VMEM, VMEM) if last else VMEM,
        scratch_shapes=[buffer, buffer] + ([pltpu.VMEM((6 * CY, 256), f32)] if last else []),
        compiler_params=PARAMS,
        cost_estimate=pl.CostEstimate(flops=40_000_000, bytes_accessed=2_000_000, transcendentals=0),
        name="fine_last" if last else "fine_steps",
    )(left, mid, right, *([oc] if last else []))


def first_coarse_kernel(left_ref, mid_ref, right_ref, out_ref, a, b, sums):
    group, slab = position()
    for c in range(3):
        for part, ref in enumerate((left_ref, mid_ref, right_ref)):
            rows = restricted(lambda c, p, start: ref[c, p, pl.ds(start, 32, stride=2), :])
            for p in range(2):
                sums[pl.ds((c * 6 + part * 2 + p) * CY, CY), :] = rows(c, p)
    averaged = dot(sums[...], pairs_to_one(0.125))
    for c in range(3):
        for i in range(6):
            at = (c * 6 + i) * CY
            a[c, i] = averaged[at : at + CY]
    has_left = jnp.where(slab > 0, f32(1.0), f32(0.0))
    has_right = jnp.where(slab < SLABS - 1, f32(1.0), f32(0.0))
    limits = lambda i: has_left if i < 2 else has_right if i >= 4 else None
    coarse_step(reads(a), writes(b), 1, 5, limits)
    into = writes(out_ref)
    coarse_step(reads(b), lambda c, i, j, value: into(c, i - 2, j, value), 2, 4, limits)


def first_coarse(left, mid, right):
    buffer = pltpu.VMEM((3, 6, CY, NZ), f32)
    return pl.pallas_call(
        first_coarse_kernel,
        out_shape=jax.ShapeDtypeStruct((3, 2, CY, NZ), f32),
        in_specs=[VMEM, VMEM, VMEM],
        out_specs=VMEM,
        scratch_shapes=[buffer, buffer, pltpu.VMEM((18 * CY, 256), f32)],
        compiler_params=PARAMS,
        cost_estimate=pl.CostEstimate(flops=4_000_000, bytes_accessed=1_300_000, transcendentals=0),
        name="first_coarse",
    )(left, mid, right)


def change_kernel(ends_ref, oc_ref, out_ref):
    expand = one_to_pairs()
    for c in range(3):
        for p in range(2):
            wide = dot(oc_ref[c, p], expand)
            tall = jnp.concatenate([wide[:, :NZ], wide[:, NZ:]], axis=0)
            for i in (2 * p, 2 * p + 1):
                for start in (0, 1):
                    at = pl.ds(start, 32, stride=2)
                    out_ref[c, i, at, :] = ends_ref[c, i, at, :] - tall


def fine_change(ends, oc):
    return pl.pallas_call(
        change_kernel,
        out_shape=jax.ShapeDtypeStruct(ends.shape, f32),
        in_specs=[VMEM, VMEM],
        out_specs=VMEM,
        compiler_params=PARAMS,
        cost_estimate=pl.CostEstimate(flops=1_000_000, bytes_accessed=900_000, transcendentals=0),
        name="fine_change",
    )(ends, oc)


def halves(count):
    outer = count - 2
    first = min(outer, 4)
    for i in range(first):
        yield 0, i, outer - first + i
        yield 1, i, outer + 4 + i
    for i in range(outer - first):
        yield 0, first + i, i
        yield 1, first + i, outer + 4 + first + i
    for i in range(2):
        yield 0, outer + i, outer + i
        yield 1, outer + i, outer + 2 + i


def sweep_kernel(target, depth, *refs):
    got_ref, before_ref, own_ref, *kept = refs[: 3 + depth]
    state_ref, *results = refs[3 + depth : 4 + 2 * depth]
    a, b = refs[4 + 2 * depth :]
    group, slab = position()
    core = slab & 1
    mine = group == target
    reach = 2 * depth
    width = 2 * reach + 4
    source = {place: (core_at, at) for core_at, at, place in halves(reach + 2)}

    def got(c, i, j):
        core_at, at = source[i]
        return got_ref[core_at, c, at, 8 * j : 8 * j + 8, :]

    chip = slab >> 1
    inside = {}
    for k in range(-reach, reach + 4):
        block = k // 4
        if block not in inside:
            there = chip + block
            inside[block] = None if block == 0 else jnp.where((there >= 0) & (there < SLABS // 2), f32(1.0), f32(0.0))
    limits = lambda i: inside[(i - reach) // 4]
    at_before = 0
    for turn in range(depth):
        edge = 2 * turn
        coarse_step(reads(a) if turn else got, writes(b), edge + 1, width - edge - 1, limits)
        coarse_step(reads(b), writes(a), edge + 2, width - edge - 2, limits)
        for c in range(3):
            for i in range(2):
                value = jnp.where(core == 0, a[c, reach + i], a[c, reach + 2 + i])
                results[turn][c, i] = jnp.where(mine, value, kept[turn][c, i])
        if turn == depth - 1:
            for c in range(3):
                for i in range(4):
                    state_ref[c, i] = a[c, reach + i] + own_ref[c, i]
        else:
            count = reach - edge
            for core_at, at, place in halves(count):
                for c in range(3):
                    i = place + edge + 2
                    a[c, i] = a[c, i] + before_ref[core_at, c, at_before + at]
            at_before += count


def sweep(target, depth, got, before, own, kept):
    buffer = pltpu.VMEM((3, 4 * depth + 4, CY, NZ), f32)
    two = jax.ShapeDtypeStruct((3, 2, CY, NZ), f32)
    four = jax.ShapeDtypeStruct((3, 4, CY, NZ), f32)
    return pl.pallas_call(
        functools.partial(sweep_kernel, target, depth),
        out_shape=(four,) + (two,) * depth,
        in_specs=[VMEM] * (3 + depth),
        out_specs=(VMEM,) * (1 + depth),
        scratch_shapes=[buffer, buffer],
        compiler_params=PARAMS,
        cost_estimate=pl.CostEstimate(flops=4_000_000, bytes_accessed=900_000, transcendentals=0),
        name="sweep_%d" % depth,
    )(got, before, own, *kept)


def final_kernel(start_ref, previous_ref, own_ref, a_ref, b_ref, c_ref, out_ref):
    group, slab = position()

    @pl.when(group == 0)
    def _():
        out_ref[...] = start_ref[...]

    @pl.when(group != 0)
    def _():
        expand = one_to_pairs()
        chain = (group & 3) == 2
        for c in range(3):
            for p in range(2):
                others = a_ref[c, p] + b_ref[c, p] + c_ref[c, p]
                wide = dot(jnp.where(chain, own_ref[c, p], others), expand)
                tall = jnp.concatenate([wide[:, :NZ], wide[:, NZ:]], axis=0)
                for i in (2 * p, 2 * p + 1):
                    for start in (0, 1):
                        at = pl.ds(start, 32, stride=2)
                        out_ref[c, i, at, :] = previous_ref[c, i, at, :] + tall


def final(*arrays):
    return pl.pallas_call(
        final_kernel,
        out_shape=jax.ShapeDtypeStruct(arrays[0].shape, f32),
        in_specs=[VMEM] * len(arrays),
        out_specs=VMEM,
        compiler_params=PARAMS,
        cost_estimate=pl.CostEstimate(flops=1_000_000, bytes_accessed=1_300_000, transcendentals=0),
        name="final",
    )(*arrays)


def handed_on(value, groups, by, place):
    table = []
    for c in groups:
        for s in range(SLABS):
            if 0 <= place(s) < SLABS and 0 <= c + by < GROUPS:
                table.append((c * SLABS + s, (c + by) * SLABS + place(s)))
    return lax.ppermute(value, AXES, table)


def outward(chips):
    return lambda s: s + 2 * chips if s % 2 == 0 else s - 2 * chips


def here(s):
    return s


def both_cores(value):
    return lax.all_gather(value, "space", axis=0, tiled=False, axis_index_groups=PAIRS)


def joined(*parts):
    return jnp.concatenate(parts, axis=1)


def after(value, *others):
    return lax.optimization_barrier((value, *others))[0]


def shards(starts):
    initial = starts[0]
    slab = lax.axis_index("space")
    core = slab & 1
    up = [(s, s + 1) for s in range(SLABS - 1)]
    down = [(s + 1, s) for s in range(SLABS - 1)]
    field = initial
    for turn in range(ROUNDS):
        left = lax.ppermute(field, "space", up)
        right = lax.ppermute(field, "space", down)
        if turn == 0:
            oc = first_coarse(left, field, right)
        if turn < ROUNDS - 1:
            field = fine_round(left, field, right)
        else:
            ends, mine = fine_round(left, field, right, oc)
    pair = both_cores(mine)
    whole = joined(pair[0], pair[1])

    def near(value):
        return jnp.where(core == 0, value[:, 2:4], value[:, 0:2])

    s1 = handed_on(whole, [0], 2, outward(1))
    s0 = handed_on(mine, [0], 2, here)
    d1 = handed_on(near(whole), [1], 1, outward(1))
    d0 = handed_on(mine, [1], 1, here)
    sources = [c for c in range(3, GROUPS - 2) if c % 4 != 2]
    l1 = handed_on(whole, sources, 0, outward(1))
    l2 = handed_on(near(whole), sources[::3], 0, outward(2))
    y3 = handed_on(joined(l1, l2, mine), sources[::3], 3, here)
    y2 = handed_on(joined(l1, mine), sources[1::3], 2, here)
    y1 = handed_on(joined(near(l1), mine), sources[2::3], 1, here)
    both = both_cores(joined(s1, s0, d1, d0))
    state, own, plus = sweep(2, 2, both[:, :, :6], both[:, :, 6:], whole, (oc, oc))
    minus2 = minus1 = oc
    before = None
    for target in (6, 10, 14):
        half = jnp.where(core == 0, state[:, :2], state[:, 2:])
        s2 = handed_on(state, [target - 4], 4, outward(2))
        s1 = handed_on(state, [target - 4], 4, outward(1))
        s0 = handed_on(half, [target - 4], 4, here)
        if before is None:
            before = both_cores(joined(after(y3, state), y2, y1))
            change = after(fine_change(ends, oc), before)
            previous = handed_on(change, range(GROUPS), 1, here)
            s1 = after(s1, before)
        both = both_cores(joined(s1, s2, s0))
        state, minus2, minus1, own, plus = sweep(target, 4, both, before, whole, (minus2, minus1, own, plus))
    plus = handed_on(plus, [0, 2, 6, 10, 14], 1, here)
    minus1 = handed_on(minus1, [6, 10, 14], -1, here)
    minus2 = handed_on(minus2, [6, 10, 14], -2, here)
    return final(initial, previous, own, plus, minus1, minus2)[None]


def solution(mesh):
    placed = P("cuts", None, "space", None, None)
    return jax.shard_map(shards, mesh=mesh, in_specs=(placed,), out_specs=placed, check_vma=False)
```

```python
import functools

import jax
import jax.numpy as jnp
from jax import lax
from jax.experimental import pallas as pl
from jax.experimental.pallas import tpu as pltpu
from jax.sharding import PartitionSpec as P

FSTEPS = 16
HALO = 8
OWN = 4
ROUNDS = FSTEPS // HALO
NY = 64
NZ = 128
CY = NY // 4
GROUPS = 16
SLABS = 32
AXES = ("cuts", "space")
PAIRS = [[2 * k, 2 * k + 1] for k in range(SLABS // 2)]

fine_rate = 0.08
fine_advect = 0.04
coarse_rate = 0.16
coarse_advect = 0.16

VMEM = pl.BlockSpec(memory_space=pltpu.VMEM)
PARAMS = pltpu.CompilerParams(vmem_limit_bytes=32 * 1024 * 1024)
f32 = jnp.float32


def position():
    return lax.axis_index("cuts"), lax.axis_index("space")


def one_plane(src, dst, i, rows, rate, advect, factor, left, right):
    edge = []
    for j in range(rows // 8):
        at = 8 + 8 * j
        mid = pl.ds(at, 8)
        v = [src[c, i, mid, :] for c in range(3)]
        av = [advect * v[c] for c in range(3)]
        xp, xm = rate - av[0], rate + av[0]
        yp, ym = rate - av[1], rate + av[1]
        zp = jnp.where(right, 0.0, rate - av[2])
        zm = jnp.where(left, 0.0, rate + av[2])
        row = []
        for c in range(3):
            new = v[c] * (1.0 - 6.0 * rate)
            new += xp * src[c, i + 1, mid, :] + xm * src[c, i - 1, mid, :]
            new += yp * src[c, i, pl.ds(at + 1, 8), :] + ym * src[c, i, pl.ds(at - 1, 8), :]
            new += zp * pltpu.roll(v[c], 127, 1) + zm * pltpu.roll(v[c], 1, 1)
            if factor is not None:
                new = new * factor
            dst[c, i, mid, :] = new
            row.append(new)
        edge.append(row)
    return edge[0], edge[-1]


def lanes(shape=(8, 128)):
    return lax.broadcasted_iota(jnp.int32, shape, 1)


def coarse_plane(at, put, i, factor):
    lane = lanes()
    row = lax.broadcasted_iota(jnp.int32, (8, 128), 0)
    z_first, z_last = (lane & 63) == 0, (lane & 63) == 63
    y_first, y_last = (row == 0) & (lane < 64), (row == 7) & (lane >= 64)
    row_first, row_last = row == 0, row == 7
    v = [[at(c, i, j) for j in range(2)] for c in range(3)]
    for j in range(2):
        av = [coarse_advect * v[c][j] for c in range(3)]
        xp, xm = coarse_rate - av[0], coarse_rate + av[0]
        yp, ym = coarse_rate - av[1], coarse_rate + av[1]
        if j == 0:
            ym = jnp.where(y_first, 0.0, ym)
        else:
            yp = jnp.where(y_last, 0.0, yp)
        zp = jnp.where(z_last, 0.0, coarse_rate - av[2])
        zm = jnp.where(z_first, 0.0, coarse_rate + av[2])
        for c in range(3):
            here_, other = v[c][j], v[c][1 - j]
            swapped = pltpu.roll(other, 64, 1)
            below = jnp.where(row_last, swapped if j == 0 else other, here_)
            above = jnp.where(row_first, other if j == 0 else swapped, here_)
            new = here_ * (1.0 - 6.0 * coarse_rate)
            new += xp * at(c, i + 1, j) + xm * at(c, i - 1, j)
            new += yp * pltpu.roll(above, 7, 0) + ym * pltpu.roll(below, 1, 0)
            new += zp * pltpu.roll(here_, 127, 1) + zm * pltpu.roll(here_, 1, 1)
            if factor is not None:
                new = new * factor
            put(c, i, j, new)


def reads(ref):
    return lambda c, i, j: ref[c, i, 8 * j : 8 * j + 8, :]


def writes(ref):
    def put(c, i, j, value):
        ref[c, i, 8 * j : 8 * j + 8, :] = value

    return put


def coarse_step(at, put, begin, end, limits):
    for i in range(begin, end):
        coarse_plane(at, put, i, limits(i))


def pairs_to_one(scale):
    rows = lax.broadcasted_iota(jnp.int32, (256, 128), 0)
    columns = lax.broadcasted_iota(jnp.int32, (256, 128), 1)
    return jnp.where((rows >> 1) == columns, f32(scale), f32(0.0))


def one_to_pairs():
    rows = lax.broadcasted_iota(jnp.int32, (128, 256), 0)
    columns = lax.broadcasted_iota(jnp.int32, (128, 256), 1)
    return jnp.where(rows == (columns >> 1), f32(1.0), f32(0.0))


def dot(a, b):
    return jnp.dot(a, b, precision=lax.Precision.HIGHEST, preferred_element_type=f32)


def restricted(planes):
    def rows(c, p):
        total = (planes(c, 2 * p, 0) + planes(c, 2 * p, 1)) + (planes(c, 2 * p + 1, 0) + planes(c, 2 * p + 1, 1))
        return jnp.concatenate([total[:CY], total[CY:]], axis=1)

    return rows


def fine_kernel(last, mid_ref, sibling_ref, near_ref, far_ref, beyond_ref, *rest):
    if last:
        oc_ref, out_ref, q_ref, a, b, sums = rest
    else:
        out_ref, a, b = rest
    group, slab = position()
    core = slab & 1
    lane = lanes()
    left = lane == 0
    right = lane == 127
    zero = jnp.zeros((8, 128), f32)
    width = OWN + 2 * HALO
    for c in range(3):
        for i in range(width):
            for buffer in (a, b):
                buffer[c, i, 0:8, :] = zero
                buffer[c, i, NY + 8 : NY + 16, :] = zero
        for ref, block0, block1 in ((far_ref, 0, 4), (near_ref, 1, 3), (sibling_ref, 3, 1), (beyond_ref, 4, 0)):
            at = jnp.where(core == 0, block0, block1) * OWN
            for i in range(OWN):
                a[c, at + i, 8 : NY + 8, :] = ref[c, i]
        for i in range(OWN):
            a[c, HALO + i, 8 : NY + 8, :] = mid_ref[c, i]
    inside = [
        jnp.where(slab > 1, f32(1.0), f32(0.0)),
        jnp.where(slab > 0, f32(1.0), f32(0.0)),
        None,
        jnp.where(slab < SLABS - 1, f32(1.0), f32(0.0)),
        jnp.where(slab < SLABS - 2, f32(1.0), f32(0.0)),
    ]
    src, dst = a, b
    for step in range(1, HALO + 1):
        for i in range(step, width - step):
            one_plane(src, dst, i, NY, fine_rate, fine_advect, inside[i // OWN], left, right)
        src, dst = dst, src
    for c in range(3):
        for i in range(OWN):
            out_ref[c, i] = src[c, HALO + i, 8 : NY + 8, :]
    if last:
        rows = restricted(lambda c, p, start: src[c, HALO + p, pl.ds(8 + start, 32, stride=2), :])
        for c in range(3):
            for p in range(2):
                sums[pl.ds((c * 2 + p) * CY, CY), :] = rows(c, p)
        ended = dot(sums[...], pairs_to_one(0.125))
        keep = jnp.where(group == 0, f32(0.0), f32(1.0))
        for c in range(3):
            for p in range(2):
                at = (c * 2 + p) * CY
                q_ref[c, p] = ended[at : at + CY] - keep * oc_ref[c, p]


def fine_round(fields, oc=None):
    last = oc is not None
    shape = jax.ShapeDtypeStruct(fields[0].shape, f32)
    buffer = pltpu.VMEM((3, OWN + 2 * HALO, NY + 16, NZ), f32)
    coarse = jax.ShapeDtypeStruct((3, 2, CY, NZ), f32)
    return pl.pallas_call(
        functools.partial(fine_kernel, last),
        out_shape=(shape, coarse) if last else shape,
        in_specs=[VMEM] * (6 if last else 5),
        out_specs=(VMEM, VMEM) if last else VMEM,
        scratch_shapes=[buffer, buffer] + ([pltpu.VMEM((6 * CY, 256), f32)] if last else []),
        compiler_params=PARAMS,
        cost_estimate=pl.CostEstimate(flops=120_000_000, bytes_accessed=2_800_000, transcendentals=0),
        name="fine_last" if last else "fine_steps",
    )(*fields, *([oc] if last else []))


def first_coarse_kernel(mid_ref, sibling_ref, near_ref, out_ref, a, b, sums):
    group, slab = position()
    core = slab & 1
    for c in range(3):
        for ref, part in ((mid_ref, 1), (sibling_ref, jnp.where(core == 0, 2, 0)), (near_ref, jnp.where(core == 0, 0, 2))):
            rows = restricted(lambda c, p, start: ref[c, p, pl.ds(start, 32, stride=2), :])
            for p in range(2):
                sums[c * 6 + part * 2 + p] = rows(c, p)
    averaged = dot(sums[...].reshape(18 * CY, 256), pairs_to_one(0.125))
    for c in range(3):
        for i in range(6):
            at = (c * 6 + i) * CY
            a[c, i] = averaged[at : at + CY]
    has_left = jnp.where(slab > 0, f32(1.0), f32(0.0))
    has_right = jnp.where(slab < SLABS - 1, f32(1.0), f32(0.0))
    limits = lambda i: has_left if i < 2 else has_right if i >= 4 else None
    coarse_step(reads(a), writes(b), 1, 5, limits)
    into = writes(out_ref)
    coarse_step(reads(b), lambda c, i, j, value: into(c, i - 2, j, value), 2, 4, limits)


def first_coarse(mid, sibling, near):
    buffer = pltpu.VMEM((3, 6, CY, NZ), f32)
    return pl.pallas_call(
        first_coarse_kernel,
        out_shape=jax.ShapeDtypeStruct((3, 2, CY, NZ), f32),
        in_specs=[VMEM, VMEM, VMEM],
        out_specs=VMEM,
        scratch_shapes=[buffer, buffer, pltpu.VMEM((18, CY, 256), f32)],
        compiler_params=PARAMS,
        cost_estimate=pl.CostEstimate(flops=4_000_000, bytes_accessed=1_300_000, transcendentals=0),
        name="first_coarse",
    )(mid, sibling, near)


def change_kernel(ends_ref, oc_ref, out_ref):
    expand = one_to_pairs()
    for c in range(3):
        for p in range(2):
            wide = dot(oc_ref[c, p], expand)
            tall = jnp.concatenate([wide[:, :NZ], wide[:, NZ:]], axis=0)
            for i in (2 * p, 2 * p + 1):
                for start in (0, 1):
                    at = pl.ds(start, 32, stride=2)
                    out_ref[c, i, at, :] = ends_ref[c, i, at, :] - tall


def fine_change(ends, oc):
    return pl.pallas_call(
        change_kernel,
        out_shape=jax.ShapeDtypeStruct(ends.shape, f32),
        in_specs=[VMEM, VMEM],
        out_specs=VMEM,
        compiler_params=PARAMS,
        cost_estimate=pl.CostEstimate(flops=1_000_000, bytes_accessed=900_000, transcendentals=0),
        name="fine_change",
    )(ends, oc)


def halves(count):
    outer = count - 2
    first = min(outer, 4)
    for i in range(first):
        yield 0, i, outer - first + i
        yield 1, i, outer + 4 + i
    for i in range(outer - first):
        yield 0, first + i, i
        yield 1, first + i, outer + 4 + first + i
    for i in range(2):
        yield 0, outer + i, outer + i
        yield 1, outer + i, outer + 2 + i


def sweep_kernel(target, depth, *refs):
    got_ref, before_ref, own_ref, *kept = refs[: 3 + depth]
    state_ref, *results = refs[3 + depth : 4 + 2 * depth]
    a, b = refs[4 + 2 * depth :]
    group, slab = position()
    core = slab & 1
    mine = group == target
    reach = 2 * depth
    width = 2 * reach + 4
    source = {place: (core_at, at) for core_at, at, place in halves(reach + 2)}

    def got(c, i, j):
        core_at, at = source[i]
        return got_ref[core_at, c, at, 8 * j : 8 * j + 8, :]

    chip = slab >> 1
    inside = {}
    for k in range(-reach, reach + 4):
        block = k // 4
        if block not in inside:
            there = chip + block
            inside[block] = None if block == 0 else jnp.where((there >= 0) & (there < SLABS // 2), f32(1.0), f32(0.0))
    limits = lambda i: inside[(i - reach) // 4]
    at_before = 0
    for turn in range(depth):
        edge = 2 * turn
        coarse_step(reads(a) if turn else got, writes(b), edge + 1, width - edge - 1, limits)
        coarse_step(reads(b), writes(a), edge + 2, width - edge - 2, limits)
        for c in range(3):
            for i in range(2):
                value = jnp.where(core == 0, a[c, reach + i], a[c, reach + 2 + i])
                results[turn][c, i] = jnp.where(mine, value, kept[turn][c, i])
        if turn == depth - 1:
            for c in range(3):
                for i in range(4):
                    state_ref[c, i] = a[c, reach + i] + own_ref[c, i]
        else:
            count = reach - edge
            for core_at, at, place in halves(count):
                for c in range(3):
                    i = place + edge + 2
                    a[c, i] = a[c, i] + before_ref[core_at, c, at_before + at]
            at_before += count


def sweep(target, depth, got, before, own, kept):
    buffer = pltpu.VMEM((3, 4 * depth + 4, CY, NZ), f32)
    two = jax.ShapeDtypeStruct((3, 2, CY, NZ), f32)
    four = jax.ShapeDtypeStruct((3, 4, CY, NZ), f32)
    return pl.pallas_call(
        functools.partial(sweep_kernel, target, depth),
        out_shape=(four,) + (two,) * depth,
        in_specs=[VMEM] * (3 + depth),
        out_specs=(VMEM,) * (1 + depth),
        scratch_shapes=[buffer, buffer],
        compiler_params=PARAMS,
        cost_estimate=pl.CostEstimate(flops=4_000_000, bytes_accessed=900_000, transcendentals=0),
        name="sweep_%d" % depth,
    )(got, before, own, *kept)


def final_kernel(start_ref, previous_ref, own_ref, a_ref, b_ref, c_ref, out_ref):
    group, slab = position()

    @pl.when(group == 0)
    def _():
        out_ref[...] = start_ref[...]

    @pl.when(group != 0)
    def _():
        expand = one_to_pairs()
        chain = (group & 3) == 2
        for c in range(3):
            for p in range(2):
                others = a_ref[c, p] + b_ref[c, p] + c_ref[c, p]
                wide = dot(jnp.where(chain, own_ref[c, p], others), expand)
                tall = jnp.concatenate([wide[:, :NZ], wide[:, NZ:]], axis=0)
                for i in (2 * p, 2 * p + 1):
                    for start in (0, 1):
                        at = pl.ds(start, 32, stride=2)
                        out_ref[c, i, at, :] = previous_ref[c, i, at, :] + tall


def final(*arrays):
    return pl.pallas_call(
        final_kernel,
        out_shape=jax.ShapeDtypeStruct(arrays[0].shape, f32),
        in_specs=[VMEM] * len(arrays),
        out_specs=VMEM,
        compiler_params=PARAMS,
        cost_estimate=pl.CostEstimate(flops=1_000_000, bytes_accessed=1_300_000, transcendentals=0),
        name="final",
    )(*arrays)


def handed_on(value, groups, by, place):
    table = []
    for c in groups:
        for s in range(SLABS):
            if 0 <= place(s) < SLABS and 0 <= c + by < GROUPS:
                table.append((c * SLABS + s, (c + by) * SLABS + place(s)))
    return lax.ppermute(value, AXES, table)


def outward(chips):
    return lambda s: s + 2 * chips if s % 2 == 0 else s - 2 * chips


def here(s):
    return s


def both_cores(value):
    return lax.all_gather(value, "space", axis=0, tiled=False, axis_index_groups=PAIRS)


def joined(*parts):
    return jnp.concatenate(parts, axis=1)


def after(value, *others):
    return lax.optimization_barrier((value, *others))[0]


def shards(starts):
    initial = starts[0]
    slab = lax.axis_index("space")
    core = slab & 1
    swap = [(s, s ^ 1) for s in range(SLABS)]
    across = [(s, s + 1 if s % 2 else s - 1) for s in range(1, SLABS - 1)]
    over = [(s, s + 2) for s in range(0, SLABS - 2, 2)] + [(s, s - 2) for s in range(3, SLABS, 2)]
    field = initial
    for turn in range(ROUNDS):
        near = lax.ppermute(field, "space", across)
        far = lax.ppermute(field, "space", over)
        sibling = lax.ppermute(field, "space", swap)
        beyond = lax.ppermute(near, "space", swap)
        if turn == 0:
            oc = first_coarse(field, sibling, near)
        if turn < ROUNDS - 1:
            field = fine_round((field, sibling, near, far, beyond))
        else:
            ends, mine = fine_round((field, sibling, near, far, beyond), oc)
    pair = both_cores(mine)
    whole = joined(pair[0], pair[1])

    def nearest(value):
        return jnp.where(core == 0, value[:, 2:4], value[:, 0:2])

    s1 = handed_on(whole, [0], 2, outward(1))
    s0 = handed_on(mine, [0], 2, here)
    d1 = handed_on(nearest(whole), [1], 1, outward(1))
    d0 = handed_on(mine, [1], 1, here)
    sources = [c for c in range(3, GROUPS - 2) if c % 4 != 2]
    l1 = handed_on(whole, sources, 0, outward(1))
    l2 = handed_on(nearest(whole), sources[::3], 0, outward(2))
    y3 = handed_on(joined(l1, l2, mine), sources[::3], 3, here)
    y2 = handed_on(joined(l1, mine), sources[1::3], 2, here)
    y1 = handed_on(joined(nearest(l1), mine), sources[2::3], 1, here)
    both = both_cores(joined(s1, s0, d1, d0))
    state, own, plus = sweep(2, 2, both[:, :, :6], both[:, :, 6:], whole, (oc, oc))
    minus2 = minus1 = oc
    before = None
    for target in (6, 10, 14):
        half = jnp.where(core == 0, state[:, :2], state[:, 2:])
        s2 = handed_on(state, [target - 4], 4, outward(2))
        s1 = handed_on(state, [target - 4], 4, outward(1))
        s0 = handed_on(half, [target - 4], 4, here)
        if before is None:
            before = both_cores(joined(after(y3, state), y2, y1))
            change = after(fine_change(ends, oc), before)
            previous = handed_on(change, range(GROUPS), 1, here)
            s1 = after(s1, before)
        both = both_cores(joined(s1, s2, s0))
        state, minus2, minus1, own, plus = sweep(target, 4, both, before, whole, (minus2, minus1, own, plus))
    plus = handed_on(plus, [0, 2, 6, 10, 14], 1, here)
    minus1 = handed_on(minus1, [6, 10, 14], -1, here)
    minus2 = handed_on(minus2, [6, 10, 14], -2, here)
    return final(initial, previous, own, plus, minus1, minus2)[None]


def solution(mesh):
    placed = P("cuts", None, "space", None, None)
    return jax.shard_map(shards, mesh=mesh, in_specs=(placed,), out_specs=placed, check_vma=False)
```

```python
import functools

import jax
import jax.numpy as jnp
from jax import lax
from jax.experimental import pallas as pl
from jax.experimental.pallas import tpu as pltpu
from jax.sharding import PartitionSpec as P

FSTEPS = 16
HALO = 8
OWN = 4
ROUNDS = FSTEPS // HALO
NY = 64
NZ = 128
CY = NY // 4
GROUPS = 16
SLABS = 32
AXES = ("cuts", "space")
PAIRS = [[2 * k, 2 * k + 1] for k in range(SLABS // 2)]

fine_rate = 0.08
fine_advect = 0.04
coarse_rate = 0.16
coarse_advect = 0.16

VMEM = pl.BlockSpec(memory_space=pltpu.VMEM)
PARAMS = pltpu.CompilerParams(vmem_limit_bytes=32 * 1024 * 1024)
f32 = jnp.float32


def position():
    return lax.axis_index("cuts"), lax.axis_index("space")


def one_plane(src, dst, i, rows, rate, advect, factor, left, right):
    edge = []
    for j in range(rows // 8):
        at = 8 + 8 * j
        mid = pl.ds(at, 8)
        v = [src[c, i, mid, :] for c in range(3)]
        av = [advect * v[c] for c in range(3)]
        xp, xm = rate - av[0], rate + av[0]
        yp, ym = rate - av[1], rate + av[1]
        zp = jnp.where(right, 0.0, rate - av[2])
        zm = jnp.where(left, 0.0, rate + av[2])
        row = []
        for c in range(3):
            new = v[c] * (1.0 - 6.0 * rate)
            new += xp * src[c, i + 1, mid, :] + xm * src[c, i - 1, mid, :]
            new += yp * src[c, i, pl.ds(at + 1, 8), :] + ym * src[c, i, pl.ds(at - 1, 8), :]
            new += zp * pltpu.roll(v[c], 127, 1) + zm * pltpu.roll(v[c], 1, 1)
            if factor is not None:
                new = new * factor
            dst[c, i, mid, :] = new
            row.append(new)
        edge.append(row)
    return edge[0], edge[-1]


def lanes(shape=(8, 128)):
    return lax.broadcasted_iota(jnp.int32, shape, 1)


def coarse_plane(at, put, i, factor):
    lane = lanes()
    row = lax.broadcasted_iota(jnp.int32, (8, 128), 0)
    z_first, z_last = (lane & 63) == 0, (lane & 63) == 63
    y_first, y_last = (row == 0) & (lane < 64), (row == 7) & (lane >= 64)
    row_first, row_last = row == 0, row == 7
    v = [[at(c, i, j) for j in range(2)] for c in range(3)]
    for j in range(2):
        av = [coarse_advect * v[c][j] for c in range(3)]
        xp, xm = coarse_rate - av[0], coarse_rate + av[0]
        yp, ym = coarse_rate - av[1], coarse_rate + av[1]
        if j == 0:
            ym = jnp.where(y_first, 0.0, ym)
        else:
            yp = jnp.where(y_last, 0.0, yp)
        zp = jnp.where(z_last, 0.0, coarse_rate - av[2])
        zm = jnp.where(z_first, 0.0, coarse_rate + av[2])
        for c in range(3):
            here_, other = v[c][j], v[c][1 - j]
            swapped = pltpu.roll(other, 64, 1)
            below = jnp.where(row_last, swapped if j == 0 else other, here_)
            above = jnp.where(row_first, other if j == 0 else swapped, here_)
            new = here_ * (1.0 - 6.0 * coarse_rate)
            new += xp * at(c, i + 1, j) + xm * at(c, i - 1, j)
            new += yp * pltpu.roll(above, 7, 0) + ym * pltpu.roll(below, 1, 0)
            new += zp * pltpu.roll(here_, 127, 1) + zm * pltpu.roll(here_, 1, 1)
            if factor is not None:
                new = new * factor
            put(c, i, j, new)


def reads(ref):
    return lambda c, i, j: ref[c, i, 8 * j : 8 * j + 8, :]


def writes(ref):
    def put(c, i, j, value):
        ref[c, i, 8 * j : 8 * j + 8, :] = value

    return put


def coarse_step(at, put, begin, end, limits):
    for i in range(begin, end):
        coarse_plane(at, put, i, limits(i))


def pairs_to_one(scale):
    rows = lax.broadcasted_iota(jnp.int32, (256, 128), 0)
    columns = lax.broadcasted_iota(jnp.int32, (256, 128), 1)
    return jnp.where((rows >> 1) == columns, f32(scale), f32(0.0))


def one_to_pairs():
    rows = lax.broadcasted_iota(jnp.int32, (128, 256), 0)
    columns = lax.broadcasted_iota(jnp.int32, (128, 256), 1)
    return jnp.where(rows == (columns >> 1), f32(1.0), f32(0.0))


def dot(a, b):
    return jnp.dot(a, b, precision=lax.Precision.HIGHEST, preferred_element_type=f32)


def restricted(planes):
    def rows(c, p):
        total = (planes(c, 2 * p, 0) + planes(c, 2 * p, 1)) + (planes(c, 2 * p + 1, 0) + planes(c, 2 * p + 1, 1))
        return jnp.concatenate([total[:CY], total[CY:]], axis=1)

    return rows


def fine_kernel(last, mid_ref, sibling_ref, near_ref, far_ref, beyond_ref, *rest):
    if last:
        oc_ref, out_ref, q_ref, a, b, sums = rest
    else:
        out_ref, a, b = rest
    group, slab = position()
    core = slab & 1
    lane = lanes()
    left = lane == 0
    right = lane == 127
    zero = jnp.zeros((8, 128), f32)
    width = OWN + 2 * HALO
    for c in range(3):
        for i in range(width):
            for buffer in (a, b):
                buffer[c, i, 0:8, :] = zero
                buffer[c, i, NY + 8 : NY + 16, :] = zero
        for ref, block0, block1 in ((far_ref, 0, 4), (near_ref, 1, 3), (sibling_ref, 3, 1), (beyond_ref, 4, 0)):
            at = jnp.where(core == 0, block0, block1) * OWN
            for i in range(OWN):
                a[c, at + i, 8 : NY + 8, :] = ref[c, i]
        for i in range(OWN):
            a[c, HALO + i, 8 : NY + 8, :] = mid_ref[c, i]
    inside = [
        jnp.where(slab > 1, f32(1.0), f32(0.0)),
        jnp.where(slab > 0, f32(1.0), f32(0.0)),
        None,
        jnp.where(slab < SLABS - 1, f32(1.0), f32(0.0)),
        jnp.where(slab < SLABS - 2, f32(1.0), f32(0.0)),
    ]
    src, dst = a, b
    for step in range(1, HALO + 1):
        for i in range(step, width - step):
            one_plane(src, dst, i, NY, fine_rate, fine_advect, inside[i // OWN], left, right)
        src, dst = dst, src
    for c in range(3):
        for i in range(OWN):
            out_ref[c, i] = src[c, HALO + i, 8 : NY + 8, :]
    if last:
        rows = restricted(lambda c, p, start: src[c, HALO + p, pl.ds(8 + start, 32, stride=2), :])
        for c in range(3):
            for p in range(2):
                sums[pl.ds((c * 2 + p) * CY, CY), :] = rows(c, p)
        ended = dot(sums[...], pairs_to_one(0.125))
        keep = jnp.where(group == 0, f32(0.0), f32(1.0))
        for c in range(3):
            for p in range(2):
                at = (c * 2 + p) * CY
                q_ref[c, p] = ended[at : at + CY] - keep * oc_ref[c, p]


def fine_round(fields, oc=None):
    last = oc is not None
    shape = jax.ShapeDtypeStruct(fields[0].shape, f32)
    buffer = pltpu.VMEM((3, OWN + 2 * HALO, NY + 16, NZ), f32)
    coarse = jax.ShapeDtypeStruct((3, 2, CY, NZ), f32)
    return pl.pallas_call(
        functools.partial(fine_kernel, last),
        out_shape=(shape, coarse) if last else shape,
        in_specs=[VMEM] * (6 if last else 5),
        out_specs=(VMEM, VMEM) if last else VMEM,
        scratch_shapes=[buffer, buffer] + ([pltpu.VMEM((6 * CY, 256), f32)] if last else []),
        compiler_params=PARAMS,
        cost_estimate=pl.CostEstimate(flops=120_000_000, bytes_accessed=2_800_000, transcendentals=0),
        name="fine_last" if last else "fine_steps",
    )(*fields, *([oc] if last else []))


def first_coarse_kernel(mid_ref, sibling_ref, near_ref, out_ref, a, b, sums):
    group, slab = position()
    core = slab & 1
    for c in range(3):
        for ref, part in ((mid_ref, 1), (sibling_ref, jnp.where(core == 0, 2, 0)), (near_ref, jnp.where(core == 0, 0, 2))):
            rows = restricted(lambda c, p, start: ref[c, p, pl.ds(start, 32, stride=2), :])
            for p in range(2):
                sums[c * 6 + part * 2 + p] = rows(c, p)
    averaged = dot(sums[...].reshape(18 * CY, 256), pairs_to_one(0.125))
    for c in range(3):
        for i in range(6):
            at = (c * 6 + i) * CY
            a[c, i] = averaged[at : at + CY]
    has_left = jnp.where(slab > 0, f32(1.0), f32(0.0))
    has_right = jnp.where(slab < SLABS - 1, f32(1.0), f32(0.0))
    limits = lambda i: has_left if i < 2 else has_right if i >= 4 else None
    coarse_step(reads(a), writes(b), 1, 5, limits)
    into = writes(out_ref)
    coarse_step(reads(b), lambda c, i, j, value: into(c, i - 2, j, value), 2, 4, limits)


def first_coarse(mid, sibling, near):
    buffer = pltpu.VMEM((3, 6, CY, NZ), f32)
    return pl.pallas_call(
        first_coarse_kernel,
        out_shape=jax.ShapeDtypeStruct((3, 2, CY, NZ), f32),
        in_specs=[VMEM, VMEM, VMEM],
        out_specs=VMEM,
        scratch_shapes=[buffer, buffer, pltpu.VMEM((18, CY, 256), f32)],
        compiler_params=PARAMS,
        cost_estimate=pl.CostEstimate(flops=4_000_000, bytes_accessed=1_300_000, transcendentals=0),
        name="first_coarse",
    )(mid, sibling, near)


def change_kernel(ends_ref, oc_ref, out_ref):
    expand = one_to_pairs()
    for c in range(3):
        for p in range(2):
            wide = dot(oc_ref[c, p], expand)
            tall = jnp.concatenate([wide[:, :NZ], wide[:, NZ:]], axis=0)
            for i in (2 * p, 2 * p + 1):
                for start in (0, 1):
                    at = pl.ds(start, 32, stride=2)
                    out_ref[c, i, at, :] = ends_ref[c, i, at, :] - tall


def fine_change(ends, oc):
    return pl.pallas_call(
        change_kernel,
        out_shape=jax.ShapeDtypeStruct(ends.shape, f32),
        in_specs=[VMEM, VMEM],
        out_specs=VMEM,
        compiler_params=PARAMS,
        cost_estimate=pl.CostEstimate(flops=1_000_000, bytes_accessed=900_000, transcendentals=0),
        name="fine_change",
    )(ends, oc)


def halves(count):
    outer = count - 2
    first = min(outer, 4)
    for i in range(first):
        yield 0, i, outer - first + i
        yield 1, i, outer + 4 + i
    for i in range(outer - first):
        yield 0, first + i, i
        yield 1, first + i, outer + 4 + first + i
    for i in range(2):
        yield 0, outer + i, outer + i
        yield 1, outer + i, outer + 2 + i


def sweep_kernel(target, depth, *refs):
    got_ref, before_ref, *kept = refs[: 2 + depth]
    state_ref, half_ref, *results = refs[2 + depth : 4 + 2 * depth]
    a, b = refs[4 + 2 * depth :]
    group, slab = position()
    core = slab & 1
    mine = group == target
    reach = 2 * depth
    width = 2 * reach + 4
    source = {place: (core_at, at) for core_at, at, place in halves(reach + 2)}

    def got(c, i, j):
        core_at, at = source[i]
        return got_ref[core_at, c, at, 8 * j : 8 * j + 8, :]

    chip = slab >> 1
    inside = {}
    for k in range(-reach, reach + 4):
        block = k // 4
        if block not in inside:
            there = chip + block
            inside[block] = None if block == 0 else jnp.where((there >= 0) & (there < SLABS // 2), f32(1.0), f32(0.0))
    limits = lambda i: inside[(i - reach) // 4]
    at_before = 0
    for turn in range(depth):
        edge = 2 * turn
        coarse_step(reads(a) if turn else got, writes(b), edge + 1, width - edge - 1, limits)
        coarse_step(reads(b), writes(a), edge + 2, width - edge - 2, limits)
        for c in range(3):
            for i in range(2):
                value = jnp.where(core == 0, a[c, reach + i], a[c, reach + 2 + i])
                results[turn][c, i] = jnp.where(mine, value, kept[turn][c, i])
        count = reach - edge
        for core_at, at, place in halves(count):
            for c in range(3):
                i = place + edge + 2
                a[c, i] = a[c, i] + before_ref[core_at, c, at_before + at]
        at_before += count
    for c in range(3):
        for i in range(4):
            state_ref[c, i] = a[c, reach + i]
        for i in range(2):
            half_ref[c, i] = jnp.where(core == 0, a[c, reach + i], a[c, reach + 2 + i])


def sweep(target, depth, got, before, kept):
    buffer = pltpu.VMEM((3, 4 * depth + 4, CY, NZ), f32)
    two = jax.ShapeDtypeStruct((3, 2, CY, NZ), f32)
    four = jax.ShapeDtypeStruct((3, 4, CY, NZ), f32)
    return pl.pallas_call(
        functools.partial(sweep_kernel, target, depth),
        out_shape=(four, two) + (two,) * depth,
        in_specs=[VMEM] * (2 + depth),
        out_specs=(VMEM,) * (2 + depth),
        scratch_shapes=[buffer, buffer],
        compiler_params=PARAMS,
        cost_estimate=pl.CostEstimate(flops=4_000_000, bytes_accessed=900_000, transcendentals=0),
        name="sweep_%d" % depth,
    )(got, before, *kept)


def final_kernel(start_ref, previous_ref, own_ref, a_ref, b_ref, c_ref, out_ref):
    group, slab = position()

    @pl.when(group == 0)
    def _():
        out_ref[...] = start_ref[...]

    @pl.when(group != 0)
    def _():
        expand = one_to_pairs()
        chain = (group == 2) | ((group & 3) == 0)
        for c in range(3):
            for p in range(2):
                others = a_ref[c, p] + b_ref[c, p] + c_ref[c, p]
                wide = dot(jnp.where(chain, own_ref[c, p], others), expand)
                tall = jnp.concatenate([wide[:, :NZ], wide[:, NZ:]], axis=0)
                for i in (2 * p, 2 * p + 1):
                    for start in (0, 1):
                        at = pl.ds(start, 32, stride=2)
                        out_ref[c, i, at, :] = previous_ref[c, i, at, :] + tall


def final(*arrays):
    return pl.pallas_call(
        final_kernel,
        out_shape=jax.ShapeDtypeStruct(arrays[0].shape, f32),
        in_specs=[VMEM] * len(arrays),
        out_specs=VMEM,
        compiler_params=PARAMS,
        cost_estimate=pl.CostEstimate(flops=1_000_000, bytes_accessed=1_300_000, transcendentals=0),
        name="final",
    )(*arrays)


def legs(groups, by, place):
    table = []
    for c in groups:
        for s in range(SLABS):
            if 0 <= place(s) < SLABS and 0 <= c + by < GROUPS:
                table.append((c * SLABS + s, (c + by) * SLABS + place(s)))
    return table


def moved(value, table):
    return lax.ppermute(value, AXES, table)


def outward(chips):
    return lambda s: s + 2 * chips if s % 2 == 0 else s - 2 * chips


def here(s):
    return s


def both_cores(value):
    return lax.all_gather(value, "space", axis=0, tiled=False, axis_index_groups=PAIRS)


def joined(*parts):
    return jnp.concatenate(parts, axis=1)


def after(value, *others):
    return lax.optimization_barrier((value, *others))[0]


def shards(starts):
    initial = starts[0]
    slab = lax.axis_index("space")
    core = slab & 1
    swap = [(s, s ^ 1) for s in range(SLABS)]
    across = [(s, s + 1 if s % 2 else s - 1) for s in range(1, SLABS - 1)]
    over = [(s, s + 2) for s in range(0, SLABS - 2, 2)] + [(s, s - 2) for s in range(3, SLABS, 2)]
    field = initial
    for turn in range(ROUNDS):
        near = lax.ppermute(field, "space", across)
        far = lax.ppermute(field, "space", over)
        sibling = lax.ppermute(field, "space", swap)
        beyond = lax.ppermute(near, "space", swap)
        if turn == 0:
            oc = first_coarse(field, sibling, near)
        if turn < ROUNDS - 1:
            field = fine_round((field, sibling, near, far, beyond))
        else:
            ends, mine = fine_round((field, sibling, near, far, beyond), oc)
    pair = both_cores(mine)
    whole = joined(pair[0], pair[1])

    def nearest(value):
        return jnp.where(core == 0, value[:, 2:4], value[:, 0:2])

    sources = [c for c in range(3, GROUPS - 2) if c % 4 != 2]
    wide = moved(whole, legs([0], 2, outward(1)) + legs(sources, 0, outward(1)))
    thin = moved(nearest(whole), legs([1], 1, outward(1)) + legs([3, 7, 11], 0, outward(2)))
    inner = moved(mine, legs([0], 2, here) + legs([6, 10, 14], -2, here))
    inner1 = moved(mine, legs([1], 1, here))
    to_next = joined(wide, thin, mine)
    to_last = joined(nearest(wide), mine)
    y3 = moved(to_next, legs([3, 7, 11], 1, here))
    y1 = moved(to_last, legs([5, 9, 13], -1, here))
    wide, to_next, to_last = lax.optimization_barrier((wide, to_next, to_last))
    both = both_cores(joined(wide, inner, thin, inner1, mine))
    state, half, own, plus1 = sweep(2, 2, both[:, :, :6], both[:, :, 6:], (oc, oc))
    plus2 = plus3 = oc
    before = None
    for target, by in ((4, 2), (8, 4), (12, 4)):
        s2 = moved(state, legs([target - by], by, outward(2)))
        s1 = moved(state, legs([target - by], by, outward(1)))
        s0 = moved(half, legs([target - by], by, here))
        if before is None:
            before = both_cores(joined(after(y3, state), wide, mine, y1, inner))
            change = after(fine_change(ends, oc), before)
            previous = moved(change, legs(range(GROUPS), 1, here))
            s1 = after(s1, before)
        both = both_cores(joined(s1, s2, s0))
        state, half, own, plus1, plus2, plus3 = sweep(target, 4, both, before, (own, plus1, plus2, plus3))
    plus3 = moved(plus3, legs([4, 8, 12], 3, here))
    plus2 = moved(plus2, legs([4, 8, 12], 2, here))
    plus1 = moved(plus1, legs([0, 2, 4, 8, 12], 1, here))
    return final(initial, previous, own, plus1, plus2, plus3)[None]


def solution(mesh):
    placed = P("cuts", None, "space", None, None)
    return jax.shard_map(shards, mesh=mesh, in_specs=(placed,), out_specs=placed, check_vma=False)
```

```python
import functools

import jax
import jax.numpy as jnp
from jax import lax
from jax.experimental import pallas as pl
from jax.experimental.pallas import tpu as pltpu
from jax.sharding import PartitionSpec as P

FSTEPS = 16
HALO = 8
OWN = 4
ROUNDS = FSTEPS // HALO
NY = 64
NZ = 128
CY = NY // 4
GROUPS = 16
SLABS = 32
AXES = ("cuts", "space")
PAIRS = [[2 * k, 2 * k + 1] for k in range(SLABS // 2)]

fine_rate = 0.08
fine_advect = 0.04
coarse_rate = 0.16
coarse_advect = 0.16

VMEM = pl.BlockSpec(memory_space=pltpu.VMEM)
PARAMS = pltpu.CompilerParams(vmem_limit_bytes=32 * 1024 * 1024)
f32 = jnp.float32


def position():
    return lax.axis_index("cuts"), lax.axis_index("space")


def one_plane(src, dst, i, rows, rate, advect, factor, left, right):
    edge = []
    for j in range(rows // 8):
        at = 8 + 8 * j
        mid = pl.ds(at, 8)
        v = [src[c, i, mid, :] for c in range(3)]
        av = [advect * v[c] for c in range(3)]
        xp, xm = rate - av[0], rate + av[0]
        yp, ym = rate - av[1], rate + av[1]
        zp = jnp.where(right, 0.0, rate - av[2])
        zm = jnp.where(left, 0.0, rate + av[2])
        row = []
        for c in range(3):
            new = v[c] * (1.0 - 6.0 * rate)
            new += xp * src[c, i + 1, mid, :] + xm * src[c, i - 1, mid, :]
            new += yp * src[c, i, pl.ds(at + 1, 8), :] + ym * src[c, i, pl.ds(at - 1, 8), :]
            new += zp * pltpu.roll(v[c], 127, 1) + zm * pltpu.roll(v[c], 1, 1)
            if factor is not None:
                new = new * factor
            dst[c, i, mid, :] = new
            row.append(new)
        edge.append(row)
    return edge[0], edge[-1]


def lanes(shape=(8, 128)):
    return lax.broadcasted_iota(jnp.int32, shape, 1)


def coarse_plane(at, put, i, factor):
    lane = lanes()
    row = lax.broadcasted_iota(jnp.int32, (8, 128), 0)
    z_first, z_last = (lane & 63) == 0, (lane & 63) == 63
    y_first, y_last = (row == 0) & (lane < 64), (row == 7) & (lane >= 64)
    row_first, row_last = row == 0, row == 7
    v = [[at(c, i, j) for j in range(2)] for c in range(3)]
    for j in range(2):
        av = [coarse_advect * v[c][j] for c in range(3)]
        xp, xm = coarse_rate - av[0], coarse_rate + av[0]
        yp, ym = coarse_rate - av[1], coarse_rate + av[1]
        if j == 0:
            ym = jnp.where(y_first, 0.0, ym)
        else:
            yp = jnp.where(y_last, 0.0, yp)
        zp = jnp.where(z_last, 0.0, coarse_rate - av[2])
        zm = jnp.where(z_first, 0.0, coarse_rate + av[2])
        for c in range(3):
            here_, other = v[c][j], v[c][1 - j]
            swapped = pltpu.roll(other, 64, 1)
            below = jnp.where(row_last, swapped if j == 0 else other, here_)
            above = jnp.where(row_first, other if j == 0 else swapped, here_)
            new = here_ * (1.0 - 6.0 * coarse_rate)
            new += xp * at(c, i + 1, j) + xm * at(c, i - 1, j)
            new += yp * pltpu.roll(above, 7, 0) + ym * pltpu.roll(below, 1, 0)
            new += zp * pltpu.roll(here_, 127, 1) + zm * pltpu.roll(here_, 1, 1)
            if factor is not None:
                new = new * factor
            put(c, i, j, new)


def reads(ref):
    return lambda c, i, j: ref[c, i, 8 * j : 8 * j + 8, :]


def writes(ref):
    def put(c, i, j, value):
        ref[c, i, 8 * j : 8 * j + 8, :] = value

    return put


def coarse_step(at, put, begin, end, limits):
    for i in range(begin, end):
        coarse_plane(at, put, i, limits(i))


def pairs_to_one(scale):
    rows = lax.broadcasted_iota(jnp.int32, (256, 128), 0)
    columns = lax.broadcasted_iota(jnp.int32, (256, 128), 1)
    return jnp.where((rows >> 1) == columns, f32(scale), f32(0.0))


def one_to_pairs():
    rows = lax.broadcasted_iota(jnp.int32, (128, 256), 0)
    columns = lax.broadcasted_iota(jnp.int32, (128, 256), 1)
    return jnp.where(rows == (columns >> 1), f32(1.0), f32(0.0))


def dot(a, b):
    return jnp.dot(a, b, precision=lax.Precision.HIGHEST, preferred_element_type=f32)


def restricted(planes):
    def rows(c, p):
        total = (planes(c, 2 * p, 0) + planes(c, 2 * p, 1)) + (planes(c, 2 * p + 1, 0) + planes(c, 2 * p + 1, 1))
        return jnp.concatenate([total[:CY], total[CY:]], axis=1)

    return rows


def fine_kernel(last, mid_ref, sibling_ref, near_ref, far_ref, beyond_ref, *rest):
    if last:
        oc_ref, out_ref, q_ref, a, b, sums = rest
    else:
        out_ref, a, b = rest
    group, slab = position()
    core = slab & 1
    lane = lanes()
    left = lane == 0
    right = lane == 127
    zero = jnp.zeros((8, 128), f32)
    width = OWN + 2 * HALO
    for c in range(3):
        for i in range(width):
            for buffer in (a, b):
                buffer[c, i, 0:8, :] = zero
                buffer[c, i, NY + 8 : NY + 16, :] = zero
        for ref, block0, block1 in ((far_ref, 0, 4), (near_ref, 1, 3), (sibling_ref, 3, 1), (beyond_ref, 4, 0)):
            at = jnp.where(core == 0, block0, block1) * OWN
            for i in range(OWN):
                a[c, at + i, 8 : NY + 8, :] = ref[c, i]
        for i in range(OWN):
            a[c, HALO + i, 8 : NY + 8, :] = mid_ref[c, i]
    inside = [
        jnp.where(slab > 1, f32(1.0), f32(0.0)),
        jnp.where(slab > 0, f32(1.0), f32(0.0)),
        None,
        jnp.where(slab < SLABS - 1, f32(1.0), f32(0.0)),
        jnp.where(slab < SLABS - 2, f32(1.0), f32(0.0)),
    ]
    src, dst = a, b
    for step in range(1, HALO + 1):
        for i in range(step, width - step):
            one_plane(src, dst, i, NY, fine_rate, fine_advect, inside[i // OWN], left, right)
        src, dst = dst, src
    for c in range(3):
        for i in range(OWN):
            out_ref[c, i] = src[c, HALO + i, 8 : NY + 8, :]
    if last:
        rows = restricted(lambda c, p, start: src[c, HALO + p, pl.ds(8 + start, 32, stride=2), :])
        for c in range(3):
            for p in range(2):
                sums[pl.ds((c * 2 + p) * CY, CY), :] = rows(c, p)
        ended = dot(sums[...], pairs_to_one(0.125))
        keep = jnp.where(group == 0, f32(0.0), f32(1.0))
        for c in range(3):
            for p in range(2):
                at = (c * 2 + p) * CY
                q_ref[c, p] = ended[at : at + CY] - keep * oc_ref[c, p]


def fine_round(fields, oc=None):
    last = oc is not None
    shape = jax.ShapeDtypeStruct(fields[0].shape, f32)
    buffer = pltpu.VMEM((3, OWN + 2 * HALO, NY + 16, NZ), f32)
    coarse = jax.ShapeDtypeStruct((3, 2, CY, NZ), f32)
    return pl.pallas_call(
        functools.partial(fine_kernel, last),
        out_shape=(shape, coarse) if last else shape,
        in_specs=[VMEM] * (6 if last else 5),
        out_specs=(VMEM, VMEM) if last else VMEM,
        scratch_shapes=[buffer, buffer] + ([pltpu.VMEM((6 * CY, 256), f32)] if last else []),
        compiler_params=PARAMS,
        cost_estimate=pl.CostEstimate(flops=120_000_000, bytes_accessed=2_800_000, transcendentals=0),
        name="fine_last" if last else "fine_steps",
    )(*fields, *([oc] if last else []))


def first_coarse_kernel(mid_ref, sibling_ref, near_ref, out_ref, a, b, sums):
    group, slab = position()
    core = slab & 1
    for c in range(3):
        for ref, part in ((mid_ref, 1), (sibling_ref, jnp.where(core == 0, 2, 0)), (near_ref, jnp.where(core == 0, 0, 2))):
            rows = restricted(lambda c, p, start: ref[c, p, pl.ds(start, 32, stride=2), :])
            for p in range(2):
                sums[c * 6 + part * 2 + p] = rows(c, p)
    averaged = dot(sums[...].reshape(18 * CY, 256), pairs_to_one(0.125))
    for c in range(3):
        for i in range(6):
            at = (c * 6 + i) * CY
            a[c, i] = averaged[at : at + CY]
    has_left = jnp.where(slab > 0, f32(1.0), f32(0.0))
    has_right = jnp.where(slab < SLABS - 1, f32(1.0), f32(0.0))
    limits = lambda i: has_left if i < 2 else has_right if i >= 4 else None
    coarse_step(reads(a), writes(b), 1, 5, limits)
    into = writes(out_ref)
    coarse_step(reads(b), lambda c, i, j, value: into(c, i - 2, j, value), 2, 4, limits)


def first_coarse(mid, sibling, near):
    buffer = pltpu.VMEM((3, 6, CY, NZ), f32)
    return pl.pallas_call(
        first_coarse_kernel,
        out_shape=jax.ShapeDtypeStruct((3, 2, CY, NZ), f32),
        in_specs=[VMEM, VMEM, VMEM],
        out_specs=VMEM,
        scratch_shapes=[buffer, buffer, pltpu.VMEM((18, CY, 256), f32)],
        compiler_params=PARAMS,
        cost_estimate=pl.CostEstimate(flops=4_000_000, bytes_accessed=1_300_000, transcendentals=0),
        name="first_coarse",
    )(mid, sibling, near)


def change_kernel(ends_ref, oc_ref, out_ref):
    expand = one_to_pairs()
    for c in range(3):
        for p in range(2):
            wide = dot(oc_ref[c, p], expand)
            tall = jnp.concatenate([wide[:, :NZ], wide[:, NZ:]], axis=0)
            for i in (2 * p, 2 * p + 1):
                for start in (0, 1):
                    at = pl.ds(start, 32, stride=2)
                    out_ref[c, i, at, :] = ends_ref[c, i, at, :] - tall


def fine_change(ends, oc):
    return pl.pallas_call(
        change_kernel,
        out_shape=jax.ShapeDtypeStruct(ends.shape, f32),
        in_specs=[VMEM, VMEM],
        out_specs=VMEM,
        compiler_params=PARAMS,
        cost_estimate=pl.CostEstimate(flops=1_000_000, bytes_accessed=900_000, transcendentals=0),
        name="fine_change",
    )(ends, oc)


def halves(count):
    outer = count - 2
    first = min(outer, 4)
    for i in range(first):
        yield 0, i, outer - first + i
        yield 1, i, outer + 4 + i
    for i in range(outer - first):
        yield 0, first + i, i
        yield 1, first + i, outer + 4 + first + i
    for i in range(2):
        yield 0, outer + i, outer + i
        yield 1, outer + i, outer + 2 + i


def sweep_kernel(target, depth, *refs):
    got_ref, before_ref, *kept = refs[: 2 + depth]
    state_ref, half_ref, *results = refs[2 + depth : 4 + 2 * depth]
    a, b = refs[4 + 2 * depth :]
    group, slab = position()
    core = slab & 1
    mine = group == target
    reach = 2 * depth
    width = 2 * reach + 4
    source = {place: (core_at, at) for core_at, at, place in halves(reach + 2)}

    def got(c, i, j):
        core_at, at = source[i]
        return got_ref[core_at, c, at, 8 * j : 8 * j + 8, :]

    chip = slab >> 1
    inside = {}
    for k in range(-reach, reach + 4):
        block = k // 4
        if block not in inside:
            there = chip + block
            inside[block] = None if block == 0 else jnp.where((there >= 0) & (there < SLABS // 2), f32(1.0), f32(0.0))
    limits = lambda i: inside[(i - reach) // 4]
    at_before = 0
    for turn in range(depth):
        edge = 2 * turn
        coarse_step(reads(a) if turn else got, writes(b), edge + 1, width - edge - 1, limits)
        coarse_step(reads(b), writes(a), edge + 2, width - edge - 2, limits)
        for c in range(3):
            for i in range(2):
                value = jnp.where(core == 0, a[c, reach + i], a[c, reach + 2 + i])
                results[turn][c, i] = jnp.where(mine, value, kept[turn][c, i])
        count = reach - edge
        for core_at, at, place in halves(count):
            for c in range(3):
                i = place + edge + 2
                a[c, i] = a[c, i] + before_ref[core_at, c, at_before + at]
        at_before += count
    for c in range(3):
        for i in range(4):
            state_ref[c, i] = a[c, reach + i]
        for i in range(2):
            half_ref[c, i] = jnp.where(core == 0, a[c, reach + i], a[c, reach + 2 + i])


def sweep(target, depth, got, before, kept):
    buffer = pltpu.VMEM((3, 4 * depth + 4, CY, NZ), f32)
    two = jax.ShapeDtypeStruct((3, 2, CY, NZ), f32)
    four = jax.ShapeDtypeStruct((3, 4, CY, NZ), f32)
    return pl.pallas_call(
        functools.partial(sweep_kernel, target, depth),
        out_shape=(four, two) + (two,) * depth,
        in_specs=[VMEM] * (2 + depth),
        out_specs=(VMEM,) * (2 + depth),
        scratch_shapes=[buffer, buffer],
        compiler_params=PARAMS,
        cost_estimate=pl.CostEstimate(flops=4_000_000, bytes_accessed=900_000, transcendentals=0),
        name="sweep_%d" % depth,
    )(got, before, *kept)


def final_kernel(start_ref, low_ref, high_ref, own_ref, a_ref, b_ref, c_ref, out_ref):
    group, slab = position()

    @pl.when(group == 0)
    def _():
        out_ref[...] = start_ref[...]

    @pl.when(group != 0)
    def _():
        expand = one_to_pairs()
        chain = (group == 2) | ((group & 3) == 0)
        for c in range(3):
            for p in range(2):
                others = a_ref[c, p] + b_ref[c, p] + c_ref[c, p]
                wide = dot(jnp.where(chain, own_ref[c, p], others), expand)
                tall = jnp.concatenate([wide[:, :NZ], wide[:, NZ:]], axis=0)
                for i in (2 * p, 2 * p + 1):
                    for start in (0, 1):
                        at = pl.ds(start, 32, stride=2)
                        out_ref[c, i, at, :] = (low_ref[c, i, at, :] + high_ref[c, i, at, :]) + tall


def final(*arrays):
    return pl.pallas_call(
        final_kernel,
        out_shape=jax.ShapeDtypeStruct(arrays[0].shape, f32),
        in_specs=[VMEM] * len(arrays),
        out_specs=VMEM,
        compiler_params=PARAMS,
        cost_estimate=pl.CostEstimate(flops=1_000_000, bytes_accessed=1_300_000, transcendentals=0),
        name="final",
    )(*arrays)


def legs(groups, by, place):
    table = []
    for c in groups:
        for s in range(SLABS):
            if 0 <= place(s) < SLABS and 0 <= c + by < GROUPS:
                table.append((c * SLABS + s, (c + by) * SLABS + place(s)))
    return table


def moved(value, table):
    return lax.ppermute(value, AXES, table)


def outward(chips):
    return lambda s: s + 2 * chips if s % 2 == 0 else s - 2 * chips


def here(s):
    return s


def both_cores(value):
    return lax.all_gather(value, "space", axis=0, tiled=False, axis_index_groups=PAIRS)


def joined(*parts):
    return jnp.concatenate(parts, axis=1)


def after(value, *others):
    return lax.optimization_barrier((value, *others))[0]


def shards(starts):
    initial = starts[0]
    slab = lax.axis_index("space")
    core = slab & 1
    swap = [(s, s ^ 1) for s in range(SLABS)]
    across = [(s, s + 1 if s % 2 else s - 1) for s in range(1, SLABS - 1)]
    over = [(s, s + 2) for s in range(0, SLABS - 2, 2)] + [(s, s - 2) for s in range(3, SLABS, 2)]
    field = initial
    for turn in range(ROUNDS):
        near = lax.ppermute(field, "space", across)
        far = lax.ppermute(field, "space", over)
        sibling = lax.ppermute(field, "space", swap)
        beyond = lax.ppermute(near, "space", swap)
        if turn == 0:
            oc = first_coarse(field, sibling, near)
        if turn < ROUNDS - 1:
            field = fine_round((field, sibling, near, far, beyond))
        else:
            ends, mine = fine_round((field, sibling, near, far, beyond), oc)
    pair = both_cores(mine)
    whole = joined(pair[0], pair[1])

    def nearest(value):
        return jnp.where(core == 0, value[:, 2:4], value[:, 0:2])

    sources = [c for c in range(3, GROUPS - 2) if c % 4 != 2]
    wide = moved(whole, legs([0], 2, outward(1)) + legs(sources, 0, outward(1)))
    thin = moved(nearest(whole), legs([1], 1, outward(1)) + legs([3, 7, 11], 0, outward(2)))
    inner = moved(mine, legs([0], 2, here) + legs([6, 10, 14], -2, here))
    inner1 = moved(mine, legs([1], 1, here))
    to_next = joined(wide, thin, mine)
    to_last = joined(nearest(wide), mine)
    y3 = moved(to_next, legs([3, 7, 11], 1, here))
    y1 = moved(to_last, legs([5, 9, 13], -1, here))
    wide, to_next, to_last = lax.optimization_barrier((wide, to_next, to_last))
    both = both_cores(joined(wide, inner, thin, inner1, mine))
    state, half, own, plus1 = sweep(2, 2, both[:, :, :6], both[:, :, 6:], (oc, oc))
    plus2 = plus3 = oc
    for target, by in ((4, 2), (8, 4), (12, 4)):
        s2 = moved(state, legs([target - by], by, outward(2)))
        s1 = moved(state, legs([target - by], by, outward(1)))
        s0 = moved(half, legs([target - by], by, here))
        if target == 4:
            before = both_cores(joined(after(y3, state), wide, mine, y1, inner))
            change = after(fine_change(ends, oc), before)
            high = moved(change, legs(range(GROUPS // 2, GROUPS), 1, here))
            s1 = after(s1, before)
        both = both_cores(joined(s1, s2, s0))
        if target == 12:
            low = moved(after(change, both), legs(range(GROUPS // 2), 1, here))
        state, half, own, plus1, plus2, plus3 = sweep(target, 4, both, before, (own, plus1, plus2, plus3))
    plus3 = moved(plus3, legs([4, 8, 12], 3, here))
    plus2 = moved(plus2, legs([4, 8, 12], 2, here))
    plus1 = moved(plus1, legs([0, 2, 4, 8, 12], 1, here))
    return final(initial, low, high, own, plus1, plus2, plus3)[None]


def solution(mesh):
    placed = P("cuts", None, "space", None, None)
    return jax.shard_map(shards, mesh=mesh, in_specs=(placed,), out_specs=placed, check_vma=False)
```
